32 devices in a mesh: lon: 8 (over z, x), lat: 4 (over y, core).
Axes of the slice: x: 2, y: 2, z: 4, core: 2. Of those that a mesh axis runs over, the one named last changes fastest.
Arguments:
- ocean_state: float32 [4, 3, 512, 2048], P(None, None, 'lat', 'lon'), may hold values from -6 to 6
- mixing: float32 [3, 512, 2048], P(None, 'lat', 'lon'), may hold values from 0.1 to 1
- land_sea: int32 [512, 2048], P('lat', 'lon'), may hold values 0 or 1
Outputs:
- final_state: float32 [4, 3, 512, 2048], P(None, None, 'lat', 'lon')
The draws below stay inside these ranges and needn't reach their ends.
All inputs are finite; a program needn't handle non-finite values. No bound on the sum of `land_sea` on one device may be relied on, other than what follows from the above.
Results may differ from the reference program's by a relative error of at most 0.000029.
Values sent between devices are 32-bit elements; how exact they have to be, the bound alone decides.
A program may use at most 128 MiB of HBM per device.

```python
import math
import jax
import jax.numpy as jnp
from jax import lax

K = 3
STEPS = 8
NLAT = 512
NLON = 2048


def place_ends(values, own_key, smallest, high):
    shape = values.shape
    index_at = [jax.random.randint(jax.random.fold_in(own_key, axis), (), 0, shape[axis]) for axis in range(len(shape))]
    values = values.at[tuple(index_at)].set(smallest)
    longest = shape.index(max(shape))
    index_at[longest] = (index_at[longest] + 1) % shape[longest]
    return values.at[tuple(index_at)].set(high)


def shard_levels(rng, dims, pieces, least, high):
    loudness, own = 1.0, jax.random.fold_in(rng, 6)
    for dim, parts in pieces:
        steps = jnp.exp(jax.random.uniform(jax.random.fold_in(own, dim), (parts,), jnp.float32, least / len(pieces), high / len(pieces)))
        loudness = loudness * jnp.repeat(steps, dims[dim] // parts).reshape([-1 if axis == dim else 1 for axis in range(len(dims))])
    return loudness


def noise(key, dims, spread, bound, split=(), dtype=jnp.bfloat16):
    values = jax.random.normal(key, dims, jnp.float32) * spread
    if len(split) > 0:
        values = shard_levels(key, dims, split, -0.22, 0.18) * values
    return jnp.clip(values, min=-bound, max=bound).astype(dtype)


def setup_inputs(seed: int = 0) -> dict:
    arg_keys = jax.random.split(jax.random.key(seed), 4)
    return {
        "ocean_state": noise(arg_keys[0], (4, K, NLAT, NLON), 1.0, 6.0, ((2, 4), (3, 8)), jnp.float32),
        "mixing": jnp.clip(jnp.exp(math.log(1.0) - 2.3025851 * jax.random.uniform(arg_keys[1], (K, NLAT, NLON), jnp.float32) ** shard_levels(arg_keys[1], (K, NLAT, NLON), ((1, 4), (2, 8)), -0.2, 0.2)), 0.1, 1.0),
        "land_sea": place_ends((jax.random.randint(arg_keys[2], (NLAT, NLON), 0, 4) < 3).astype(jnp.int32), jax.random.fold_in(arg_keys[2], 1), 0, 1),
    }


THERMAL = 0.2
HALINE = 0.15
GRAVITY = 0.5
TIMESTEP = 0.1


def interior(padded, first_cut, last_cut, along):
    return lax.slice_in_dim(padded, first_cut, padded.shape[along] - last_cut, axis=along)


def flux_divergence(padded, along):
    speed_index = 2 if along == 3 else 3
    speeds = padded[speed_index:speed_index + 1]
    face_value = (7.0 * (interior(padded, 1, 2, along) + interior(padded, 2, 1, along)) - (interior(padded, 0, 3, along) + interior(padded, 3, 0, along))) / 12.0
    face_speed = 0.5 * (interior(speeds, 1, 2, along) + interior(speeds, 2, 1, along))
    face_flux = face_speed * face_value
    return interior(face_flux, 1, 0, along) - interior(face_flux, 0, 1, along)


def neighbours(padded, along):
    return interior(padded, 3, 1, along) + interior(padded, 1, 3, along)


def gradient(padded, along):
    return 0.5 * (interior(padded, 3, 1, along) - interior(padded, 1, 3, along))


def pressure(padded):
    density = -THERMAL * padded[0] + HALINE * padded[1]
    return jnp.cumsum(density, axis=0)


def advance(center, lon_padded, lat_padded, mixing, coriolis, wetness):
    advection = flux_divergence(lon_padded, 3) + flux_divergence(lat_padded, 2)
    laplacian = neighbours(lon_padded, 3) + neighbours(lat_padded, 2) - 4.0 * center
    grad_lon = gradient(pressure(lon_padded), 2)
    grad_lat = gradient(pressure(lat_padded), 1)
    tracers = center[:2]
    upper_level = jnp.concatenate([tracers[:, :1], tracers[:, :-1]], axis=1)
    lower_level = jnp.concatenate([tracers[:, 1:], tracers[:, -1:]], axis=1)
    vertical = upper_level + lower_level - 2.0 * tracers
    tracer_tend = -advection[:2] + mixing * laplacian[:2] + 0.5 * mixing * vertical
    zonal_tend = -advection[2] + coriolis * center[3] - GRAVITY * grad_lon + mixing * laplacian[2]
    merid_tend = -advection[3] - coriolis * center[2] - GRAVITY * grad_lat + mixing * laplacian[3]
    tendency = jnp.concatenate([tracer_tend, zonal_tend[None], merid_tend[None]], axis=0)
    return center + TIMESTEP * wetness * tendency


def reference(ocean_state, mixing, land_sea):
    wetness = land_sea.astype(jnp.float32)
    row_index = jnp.arange(NLAT).astype(jnp.float32)
    coriolis = jnp.sin(jnp.pi * (row_index + 0.5) / NLAT - jnp.pi / 2)[:, None]
    parity = jnp.array([1.0, 1.0, -1.0, -1.0], jnp.float32).reshape(4, 1, 1, 1)
    current = ocean_state
    for substep in range(STEPS):
        lon_padded = jnp.concatenate([current[..., -2:], current, current[..., :2]], axis=3)
        ghost_rows = current[:, :, NLAT - 2:, ::-1][:, :, ::-1, :] * parity
        south_rows = jnp.zeros_like(current[:, :, :2, :])
        lat_padded = jnp.concatenate([south_rows, current, ghost_rows], axis=2)
        current = advance(current, lon_padded, lat_padded, mixing, coriolis, wetness)
    return current
```

```python
import functools

import jax
import jax.numpy as jnp
from jax import lax
from jax.experimental import pallas as pl
from jax.experimental.pallas import tpu as pltpu
from jax.sharding import PartitionSpec as P

STEPS = 8
HALO = 2 * STEPS
FIELDS = 4
LEVELS = 3
STATE = FIELDS * LEVELS
PLANES = STATE + LEVELS + 1
SUB = 8
LANE = 128
PER_TILE = LANE // HALO
GROUPS = PLANES // PER_TILE
CHUNK = 4

THERMAL = 0.2
HALINE = 0.15
GRAVITY = 0.5
TIMESTEP = 0.1


def split3(x):
    high = x.astype(jnp.bfloat16)
    rest = x - high.astype(jnp.float32)
    mid = rest.astype(jnp.bfloat16)
    low = (rest - mid.astype(jnp.float32)).astype(jnp.bfloat16)
    return high, mid, low


def flipped(block):
    x, span = block
    rows, cols = x.shape

    def reversal(size, group):
        i = lax.broadcasted_iota(jnp.int32, (size, size), 0)
        j = lax.broadcasted_iota(jnp.int32, (size, size), 1)
        partner = (i // group) * group + (group - 1 - i % group)
        return jnp.where(j == partner, 1.0, 0.0).astype(jnp.bfloat16)

    def dot(a, b):
        return jnp.dot(a, b, preferred_element_type=jnp.float32)

    flip_lanes = reversal(cols, span)
    flip_rows = reversal(rows, HALO)
    high, mid, low = split3(x)
    x = (dot(high, flip_lanes) + dot(mid, flip_lanes)) + dot(low, flip_lanes)
    high, mid, low = split3(x)
    return (dot(flip_rows, high) + dot(flip_rows, mid)) + dot(flip_rows, low)


def exchange_kernel(
    lons, lats, state, mixing, land, north, south, west, east,
    to_west, to_east, to_north, to_south, corner_west, corner_east, send_sem, recv_sem, keep_sem,
):
    rows, cols = land.shape
    ext = rows + 2 * HALO
    lon = lax.axis_index("lon")
    lat = lax.axis_index("lat")
    northmost = lat == lats - 1
    has_south = lat > 0
    left = lax.rem(lon + lons - 1, lons)
    right = lax.rem(lon + 1, lons)
    across = lons - 1 - lon
    across_east = lax.rem(2 * lons - 2 - lon, lons)
    across_west = lax.rem(lons - lon, lons)

    barrier = pltpu.get_barrier_semaphore()

    def greet(x, y):
        pl.semaphore_signal(barrier, inc=1, device_id=(x, y), device_id_type=pl.DeviceIdType.MESH)

    greet(left, lat)
    greet(right, lat)

    @pl.when(has_south)
    def _():
        for x in (left, lon, right):
            greet(x, lat - 1)

    @pl.when(jnp.logical_not(northmost))
    def _():
        for x in (left, lon, right):
            greet(x, lat + 1)

    @pl.when(northmost)
    def _():
        greet(across, lat)

        @pl.when(across_east != lon)
        def _():
            greet(across_east, lat)

        @pl.when(across_west != lon)
        def _():
            greet(across_west, lat)

    def plane(p, row_slice, col_slice):
        if p < STATE:
            return state[p // LEVELS, p % LEVELS, row_slice, col_slice]
        if p < STATE + LEVELS:
            return mixing[p - STATE, row_slice, col_slice]
        return land[row_slice, col_slice].astype(jnp.float32)

    everything = slice(0, cols)
    for p in range(PLANES):
        to_south[p] = plane(p, slice(0, HALO), everything)
        to_north[p] = plane(p, slice(rows - HALO, rows), everything)

    lane = lax.broadcasted_iota(jnp.int32, (rows, LANE), 1)
    for g in range(GROUPS):
        packed_west = jnp.zeros((rows, LANE), jnp.float32)
        packed_east = jnp.zeros((rows, LANE), jnp.float32)
        for slot in range(PER_TILE):
            p = g * PER_TILE + slot
            here = (lane >= slot * HALO) & (lane < (slot + 1) * HALO)
            first = plane(p, slice(0, rows), slice(0, LANE))
            last = plane(p, slice(0, rows), slice(cols - LANE, cols))
            if slot:
                first = pltpu.roll(first, slot * HALO, 1)
            if (slot + 1) * HALO != LANE:
                last = pltpu.roll(last, (slot + 1) * HALO, 1)
            packed_west = jnp.where(here, first, packed_west)
            packed_east = jnp.where(here, last, packed_east)
        to_west[g] = packed_west
        to_east[g] = packed_east

    @pl.when(northmost)
    def _():
        full = to_north[...].reshape(PLANES * HALO, cols)
        index = lax.broadcasted_iota(jnp.int32, full.shape, 0) // HALO
        odd = (index >= 2 * LEVELS) & (index < STATE)
        full = flipped((full, cols))
        to_north[...] = jnp.where(odd, -full, full).reshape(PLANES, HALO, cols)
        shape = (GROUPS * HALO, LANE)
        index = (
            lax.broadcasted_iota(jnp.int32, shape, 0) // HALO * PER_TILE
            + lax.broadcasted_iota(jnp.int32, shape, 1) // HALO
        )
        odd = (index >= 2 * LEVELS) & (index < STATE)
        for source, corner in ((to_west, corner_west), (to_east, corner_east)):
            strip = flipped((source[:, rows - HALO :, :].reshape(shape), HALO))
            corner[...] = jnp.where(odd, -strip, strip).reshape(GROUPS, HALO, LANE)

    @pl.when(jnp.logical_not(northmost))
    def _():
        corner_west[...] = to_west[:, rows - HALO :, :]
        corner_east[...] = to_east[:, rows - HALO :, :]

    @pl.when(has_south & jnp.logical_not(northmost))
    def _():
        pl.semaphore_wait(barrier, 8)

    @pl.when(jnp.logical_not(has_south) & jnp.logical_not(northmost))
    def _():
        pl.semaphore_wait(barrier, 5)

    @pl.when(northmost)
    def _():
        folds = (
            1
            + (across_east != lon).astype(jnp.int32)
            + (across_west != lon).astype(jnp.int32)
        )
        pl.semaphore_wait(barrier, 2 + 3 * has_south.astype(jnp.int32) + folds)

    low = pl.ds(0, HALO)
    high = pl.ds(ext - HALO, HALO)
    middle = pl.ds(HALO, rows)

    def copy(src, dst, send, recv, x, y):
        return pltpu.make_async_remote_copy(
            src_ref=src,
            dst_ref=dst,
            send_sem=send_sem.at[send],
            recv_sem=recv_sem.at[recv],
            device_id=(x, y),
            device_id_type=pl.DeviceIdType.MESH,
        )

    def westward():
        return copy(to_west, east.at[:, middle, :], 0, 1, left, lat)

    def eastward():
        return copy(to_east, west.at[:, middle, :], 1, 0, right, lat)

    def southward():
        return (
            copy(to_south, north, 2, 2, lon, lat - 1),
            copy(to_west.at[:, low, :], east.at[:, high, :], 3, 3, left, lat - 1),
            copy(to_east.at[:, low, :], west.at[:, high, :], 4, 4, right, lat - 1),
        )

    def northward():
        return (
            copy(to_north, south, 5, 5, lon, lat + 1),
            copy(corner_west, east.at[:, low, :], 6, 6, left, lat + 1),
            copy(corner_east, west.at[:, low, :], 7, 7, right, lat + 1),
        )

    def folded():
        return copy(to_north, north, 5, 2, across, lat)

    def folded_east():
        return copy(corner_east, east.at[:, high, :], 6, 3, across_east, lat)

    def folded_west():
        return copy(corner_west, west.at[:, high, :], 7, 4, across_west, lat)

    def kept_east():
        return pltpu.make_async_copy(corner_east, east.at[:, high, :], keep_sem.at[0])

    def kept_west():
        return pltpu.make_async_copy(corner_west, west.at[:, high, :], keep_sem.at[1])

    @pl.when(has_south)
    def _():
        for c in southward():
            c.start()

    @pl.when(jnp.logical_not(northmost))
    def _():
        for c in northward():
            c.start()

    @pl.when(northmost)
    def _():
        folded().start()

        @pl.when(across_east != lon)
        def _():
            folded_east().start()

        @pl.when(across_east == lon)
        def _():
            kept_east().start()

        @pl.when(across_west != lon)
        def _():
            folded_west().start()

        @pl.when(across_west == lon)
        def _():
            kept_west().start()

    westward().start()
    eastward().start()

    @pl.when(jnp.logical_not(has_south))
    def _():
        south[...] = jnp.zeros(south.shape, jnp.float32)
        west[:, 0:HALO, :] = jnp.zeros((GROUPS, HALO, LANE), jnp.float32)
        east[:, 0:HALO, :] = jnp.zeros((GROUPS, HALO, LANE), jnp.float32)

    westward().wait()
    eastward().wait()

    @pl.when(has_south)
    def _():
        for c in southward():
            c.wait_send()
        for c in northward():
            c.wait_recv()

    @pl.when(jnp.logical_not(northmost))
    def _():
        for c in northward():
            c.wait_send()
        for c in southward():
            c.wait_recv()

    @pl.when(northmost)
    def _():
        folded().wait()

        @pl.when(across_east != lon)
        def _():
            folded_east().wait()

        @pl.when(across_east == lon)
        def _():
            kept_east().wait()

        @pl.when(across_west != lon)
        def _():
            folded_west().wait()

        @pl.when(across_west == lon)
        def _():
            kept_west().wait()


def substeps_kernel(
    lons, lats, state, mixing, land, north, south, west, east, out,
    natural, fixed, first, second, mix, wet, spin, sems, out_sem,
):
    rows, cols = land.shape
    ext = rows + 2 * HALO
    depth = ext // SUB
    wide = cols + LANE
    lat = lax.axis_index("lat")
    low, middle, high = pl.ds(0, HALO), pl.ds(HALO, rows), pl.ds(ext - HALO, HALO)

    loads = [
        c
        for t in range(cols // LANE)
        for c in (
            pltpu.make_async_copy(
                state.at[:, :, :, pl.ds(t * LANE, LANE)], natural.at[t, :, :, middle, :], sems.at[2 * t]
            ),
            pltpu.make_async_copy(
                mixing.at[:, :, pl.ds(t * LANE, LANE)],
                fixed.at[t, pl.ds(0, LEVELS), middle, :],
                sems.at[2 * t + 1],
            ),
        )
    ]
    for c in loads:
        c.start()

    r = lax.broadcasted_iota(jnp.int32, (depth, SUB, LANE), 0)
    s = lax.broadcasted_iota(jnp.int32, (depth, SUB, LANE), 1)
    total = rows * lats
    row = lat * rows - HALO + s * depth + r
    row = jnp.where(row >= total, 2 * total - 1 - row, row).astype(jnp.float32)
    turn = jnp.sin(jnp.pi * (row + 0.5) / total - jnp.pi / 2)
    for t in range(wide // LANE):
        spin[:, :, t * LANE : (t + 1) * LANE] = turn

    for t in range(cols // LANE):
        span = slice(t * LANE, (t + 1) * LANE)
        for f in range(FIELDS):
            for k in range(LEVELS):
                natural[t, f, k, 0:HALO, :] = south[f * LEVELS + k, :, span]
                natural[t, f, k, ext - HALO : ext, :] = north[f * LEVELS + k, :, span]
        for p in range(LEVELS + 1):
            fixed[t, p, 0:HALO, :] = south[STATE + p, :, span]
            fixed[t, p, ext - HALO : ext, :] = north[STATE + p, :, span]
        fixed[t, LEVELS, HALO : HALO + rows, :] = land[:, span].astype(jnp.float32)
    for c in loads:
        c.wait()

    lane = lax.broadcasted_iota(jnp.int32, (SUB, LANE), 1)

    def spread(i, carry):
        picked = pl.ds(i, SUB, stride=depth)
        wests = [west[g, picked, :] for g in range(GROUPS)]
        easts = [east[g, picked, :] for g in range(GROUPS)]
        for p in range(PLANES):
            g, slot = p // PER_TILE, p % PER_TILE
            e, w = easts[g], wests[g]
            if slot:
                e = pltpu.roll(e, LANE - slot * HALO, 1)
            if slot != PER_TILE - 1:
                w = pltpu.roll(w, LANE - (slot + 1) * HALO, 1)
            side = jnp.where(lane < HALO, e, jnp.where(lane >= LANE - HALO, w, 0.0))
            for t in range(wide // LANE):
                span = slice(t * LANE, (t + 1) * LANE)
                if t == wide // LANE - 1:
                    value = side
                elif p < STATE:
                    value = natural[t, p // LEVELS, p % LEVELS, picked, :]
                else:
                    value = fixed[t, p - STATE, picked, :]
                if p < STATE:
                    first[p, i + 2, :, span] = value
                elif p < STATE + LEVELS:
                    mix[p - STATE, i, :, span] = value
                else:
                    wet[i, :, span] = TIMESTEP * value
        return carry

    lax.fori_loop(0, depth, spread, 0)

    def ghosts(buf):
        for p in range(STATE):
            for to, source, shift in (
                (0, depth, 1), (1, depth + 1, 1), (depth + 2, 2, SUB - 1), (depth + 3, 3, SUB - 1)
            ):
                buf[p, to] = pltpu.roll(buf[p, source], shift, 0)

    def ahead(x, n):
        return pltpu.roll(x, n % wide, 1)

    def face(before, a, b, after):
        return 7.0 * (a + b) - (before + after)

    def advance(q, new):
        def rows_of(i, carry):
            base = i * CHUNK

            def at(f, k, j):
                return q[f * LEVELS + k, base + j + 2]

            def weights(j):
                total = None
                result = []
                for k in range(LEVELS):
                    density = (
                        (-THERMAL * 0.5 * GRAVITY) * at(0, k, j) + (HALINE * 0.5 * GRAVITY) * at(1, k, j)
                    )
                    total = density if total is None else total + density
                    result.append(total)
                return result

            pressures = {j: weights(j) for j in (-1, 0)}
            below = {}
            for j in range(-1, CHUNK):
                if j >= 0:
                    pressures[j + 1] = weights(j + 1)
                for k in range(LEVELS):
                    fast = (at(3, k, j) + at(3, k, j + 1)) * (1.0 / 24.0)
                    if j >= 0:
                        u = at(2, k, j)
                        along = (u + ahead(u, -1)) * (1.0 / 24.0)
                        m = mix[k, base + j]
                        a = wet[base + j]
                        turn = spin[base + j]
                        pressure = pressures[j][k]
                    for f in range(FIELDS):
                        center, next_row = at(f, k, j), at(f, k, j + 1)
                        prev_row = at(f, k, j - 1)
                        upper = fast * face(prev_row, center, next_row, at(f, k, j + 2))
                        lower = below.get((f, k))
                        below[f, k] = upper
                        if j < 0:
                            continue
                        east_1, west_1, east_2 = ahead(center, -1), ahead(center, 1), ahead(center, -2)
                        flux = along * face(west_1, center, east_1, east_2)
                        advection = (flux - ahead(flux, 1)) + (upper - lower)
                        around = (east_1 + west_1) + (next_row + prev_row)
                        if f < 2:
                            if k == 0:
                                mixed = around + (0.5 * at(f, 1, j) - 4.5 * center)
                            elif k == LEVELS - 1:
                                mixed = around + (0.5 * at(f, k - 1, j) - 4.5 * center)
                            else:
                                mixed = around + (0.5 * (at(f, k - 1, j) + at(f, k + 1, j)) - 5.0 * center)
                        else:
                            mixed = around - 4.0 * center
                        tendency = m * mixed - advection
                        if f == 2:
                            slope = ahead(pressure, -1) - ahead(pressure, 1)
                            tendency = tendency + (turn * at(3, k, j) - slope)
                        elif f == 3:
                            slope = pressures[j + 1][k] - pressures[j - 1][k]
                            tendency = tendency - (turn * at(2, k, j) + slope)
                        new[f * LEVELS + k, base + j + 2] = center + a * tendency
            return carry

        lax.fori_loop(0, depth // CHUNK, rows_of, 0)

    def pair(i, carry):
        ghosts(first)
        advance(first, second)
        ghosts(second)
        advance(second, first)
        return carry

    lax.fori_loop(0, STEPS // 2, pair, 0)

    def gather(i, carry):
        for p in range(STATE):
            for t in range(cols // LANE):
                span = slice(t * LANE, (t + 1) * LANE)
                natural[t, p // LEVELS, p % LEVELS, pl.ds(i, SUB, stride=depth), :] = first[p, i + 2, :, span]
        return carry

    lax.fori_loop(0, depth, gather, 0)
    stores = [
        pltpu.make_async_copy(
            natural.at[t, :, :, middle, :], out.at[:, :, :, pl.ds(t * LANE, LANE)], out_sem.at[t]
        )
        for t in range(cols // LANE)
    ]
    for c in stores:
        c.start()
    for c in stores:
        c.wait()


def body(lons, lats, ocean_state, mixing, land_sea):
    rows, cols = land_sea.shape
    ext, wide = rows + 2 * HALO, cols + LANE
    depth = ext // SUB
    f32 = jnp.float32
    vmem = pl.BlockSpec(memory_space=pltpu.VMEM)
    hbm = pl.BlockSpec(memory_space=pl.ANY)
    halos = pl.pallas_call(
        functools.partial(exchange_kernel, lons, lats),
        out_shape=[
            jax.ShapeDtypeStruct((PLANES, HALO, cols), f32),
            jax.ShapeDtypeStruct((PLANES, HALO, cols), f32),
            jax.ShapeDtypeStruct((GROUPS, ext, LANE), f32),
            jax.ShapeDtypeStruct((GROUPS, ext, LANE), f32),
        ],
        in_specs=[vmem] * 3,
        out_specs=[vmem] * 4,
        scratch_shapes=[
            pltpu.VMEM((GROUPS, rows, LANE), f32),
            pltpu.VMEM((GROUPS, rows, LANE), f32),
            pltpu.VMEM((PLANES, HALO, cols), f32),
            pltpu.VMEM((PLANES, HALO, cols), f32),
            pltpu.VMEM((GROUPS, HALO, LANE), f32),
            pltpu.VMEM((GROUPS, HALO, LANE), f32),
            pltpu.SemaphoreType.DMA((8,)),
            pltpu.SemaphoreType.DMA((8,)),
            pltpu.SemaphoreType.DMA((2,)),
        ],
        compiler_params=pltpu.CompilerParams(
            collective_id=0, has_side_effects=True, vmem_limit_bytes=32 * 2**20
        ),
        name="exchange",
    )(ocean_state, mixing, land_sea)
    return pl.pallas_call(
        functools.partial(substeps_kernel, lons, lats),
        out_shape=jax.ShapeDtypeStruct(ocean_state.shape, f32),
        in_specs=[hbm, hbm] + [vmem] * 5,
        out_specs=hbm,
        scratch_shapes=[
            pltpu.VMEM((cols // LANE, FIELDS, LEVELS, ext, LANE), f32),
            pltpu.VMEM((cols // LANE, LEVELS + 1, ext, LANE), f32),
            pltpu.VMEM((STATE, depth + 4, SUB, wide), f32),
            pltpu.VMEM((STATE, depth + 4, SUB, wide), f32),
            pltpu.VMEM((LEVELS, depth, SUB, wide), f32),
            pltpu.VMEM((depth, SUB, wide), f32),
            pltpu.VMEM((depth, SUB, wide), f32),
            pltpu.SemaphoreType.DMA((2 * (cols // LANE),)),
            pltpu.SemaphoreType.DMA((cols // LANE,)),
        ],
        compiler_params=pltpu.CompilerParams(vmem_limit_bytes=48 * 2**20),
        name="substeps",
    )(ocean_state, mixing, land_sea, *halos)


def solution(mesh):
    in_specs = (P(None, None, "lat", "lon"), P(None, "lat", "lon"), P("lat", "lon"))
    out_specs = P(None, None, "lat", "lon")
    run = functools.partial(body, mesh.shape["lon"], mesh.shape["lat"])
    return jax.shard_map(run, mesh=mesh, in_specs=in_specs, out_specs=out_specs, check_vma=False)
```

```python
import functools

import jax
import jax.numpy as jnp
from jax import lax
from jax.experimental import pallas as pl
from jax.experimental.pallas import tpu as pltpu
from jax.sharding import PartitionSpec as P

STEPS = 8
HALO = 2 * STEPS
FIELDS = 4
LEVELS = 3
STATE = FIELDS * LEVELS
PLANES = STATE + LEVELS + 1
SUB = 8
LANE = 128
PER_TILE = LANE // HALO
GROUPS = PLANES // PER_TILE
SIDE = 2
HALF = LANE // SIDE

THERMAL = 0.2
HALINE = 0.15
GRAVITY = 0.5
TIMESTEP = 0.1


def split3(x):
    high = x.astype(jnp.bfloat16)
    rest = x - high.astype(jnp.float32)
    mid = rest.astype(jnp.bfloat16)
    low = (rest - mid.astype(jnp.float32)).astype(jnp.bfloat16)
    return high, mid, low


def flipped(block):
    x, span = block
    rows, cols = x.shape

    def reversal(size, group):
        i = lax.broadcasted_iota(jnp.int32, (size, size), 0)
        j = lax.broadcasted_iota(jnp.int32, (size, size), 1)
        partner = (i // group) * group + (group - 1 - i % group)
        return jnp.where(j == partner, 1.0, 0.0).astype(jnp.bfloat16)

    def dot(a, b):
        return jnp.dot(a, b, preferred_element_type=jnp.float32)

    flip_lanes = reversal(cols, span)
    flip_rows = reversal(rows, HALO)
    high, mid, low = split3(x)
    x = (dot(high, flip_lanes) + dot(mid, flip_lanes)) + dot(low, flip_lanes)
    high, mid, low = split3(x)
    return (dot(flip_rows, high) + dot(flip_rows, mid)) + dot(flip_rows, low)


def exchange_kernel(
    lons, lats, state, mixing, land, north, south, west, east,
    to_west, to_east, to_north, to_south, corner_west, corner_east, send_sem, recv_sem, keep_sem,
):
    rows, cols = land.shape
    ext = rows + 2 * HALO
    lon = lax.axis_index("lon")
    lat = lax.axis_index("lat")
    northmost = lat == lats - 1
    has_south = lat > 0
    left = lax.rem(lon + lons - 1, lons)
    right = lax.rem(lon + 1, lons)
    across = lons - 1 - lon
    across_east = lax.rem(2 * lons - 2 - lon, lons)
    across_west = lax.rem(lons - lon, lons)

    barrier = pltpu.get_barrier_semaphore()

    def greet(x, y):
        pl.semaphore_signal(barrier, inc=1, device_id=(x, y), device_id_type=pl.DeviceIdType.MESH)

    greet(left, lat)
    greet(right, lat)

    @pl.when(has_south)
    def _():
        for x in (left, lon, right):
            greet(x, lat - 1)

    @pl.when(jnp.logical_not(northmost))
    def _():
        for x in (left, lon, right):
            greet(x, lat + 1)

    @pl.when(northmost)
    def _():
        greet(across, lat)

        @pl.when(across_east != lon)
        def _():
            greet(across_east, lat)

        @pl.when(across_west != lon)
        def _():
            greet(across_west, lat)

    def plane(p, row_slice, col_slice):
        if p < STATE:
            return state[p // LEVELS, p % LEVELS, row_slice, col_slice]
        if p < STATE + LEVELS:
            return mixing[p - STATE, row_slice, col_slice]
        return land[row_slice, col_slice].astype(jnp.float32)

    everything = slice(0, cols)
    for p in range(PLANES):
        to_south[p] = plane(p, slice(0, HALO), everything)
        to_north[p] = plane(p, slice(rows - HALO, rows), everything)

    lane = lax.broadcasted_iota(jnp.int32, (rows, LANE), 1)
    for g in range(GROUPS):
        packed_west = jnp.zeros((rows, LANE), jnp.float32)
        packed_east = jnp.zeros((rows, LANE), jnp.float32)
        for slot in range(PER_TILE):
            p = g * PER_TILE + slot
            here = (lane >= slot * HALO) & (lane < (slot + 1) * HALO)
            first = plane(p, slice(0, rows), slice(0, LANE))
            last = plane(p, slice(0, rows), slice(cols - LANE, cols))
            if slot:
                first = pltpu.roll(first, slot * HALO, 1)
            if (slot + 1) * HALO != LANE:
                last = pltpu.roll(last, (slot + 1) * HALO, 1)
            packed_west = jnp.where(here, first, packed_west)
            packed_east = jnp.where(here, last, packed_east)
        to_west[g] = packed_west
        to_east[g] = packed_east

    @pl.when(northmost)
    def _():
        full = to_north[...].reshape(PLANES * HALO, cols)
        index = lax.broadcasted_iota(jnp.int32, full.shape, 0) // HALO
        odd = (index >= 2 * LEVELS) & (index < STATE)
        full = flipped((full, cols))
        to_north[...] = jnp.where(odd, -full, full).reshape(PLANES, HALO, cols)
        shape = (GROUPS * HALO, LANE)
        index = (
            lax.broadcasted_iota(jnp.int32, shape, 0) // HALO * PER_TILE
            + lax.broadcasted_iota(jnp.int32, shape, 1) // HALO
        )
        odd = (index >= 2 * LEVELS) & (index < STATE)
        for source, corner in ((to_west, corner_west), (to_east, corner_east)):
            strip = flipped((source[:, rows - HALO :, :].reshape(shape), HALO))
            corner[...] = jnp.where(odd, -strip, strip).reshape(GROUPS, HALO, LANE)

    @pl.when(jnp.logical_not(northmost))
    def _():
        corner_west[...] = to_west[:, rows - HALO :, :]
        corner_east[...] = to_east[:, rows - HALO :, :]

    @pl.when(has_south & jnp.logical_not(northmost))
    def _():
        pl.semaphore_wait(barrier, 8)

    @pl.when(jnp.logical_not(has_south) & jnp.logical_not(northmost))
    def _():
        pl.semaphore_wait(barrier, 5)

    @pl.when(northmost)
    def _():
        folds = (
            1
            + (across_east != lon).astype(jnp.int32)
            + (across_west != lon).astype(jnp.int32)
        )
        pl.semaphore_wait(barrier, 2 + 3 * has_south.astype(jnp.int32) + folds)

    low = pl.ds(0, HALO)
    high = pl.ds(ext - HALO, HALO)
    middle = pl.ds(HALO, rows)

    def copy(src, dst, send, recv, x, y):
        return pltpu.make_async_remote_copy(
            src_ref=src,
            dst_ref=dst,
            send_sem=send_sem.at[send],
            recv_sem=recv_sem.at[recv],
            device_id=(x, y),
            device_id_type=pl.DeviceIdType.MESH,
        )

    def westward():
        return copy(to_west, east.at[:, middle, :], 0, 1, left, lat)

    def eastward():
        return copy(to_east, west.at[:, middle, :], 1, 0, right, lat)

    def southward():
        return (
            copy(to_south, north, 2, 2, lon, lat - 1),
            copy(to_west.at[:, low, :], east.at[:, high, :], 3, 3, left, lat - 1),
            copy(to_east.at[:, low, :], west.at[:, high, :], 4, 4, right, lat - 1),
        )

    def northward():
        return (
            copy(to_north, south, 5, 5, lon, lat + 1),
            copy(corner_west, east.at[:, low, :], 6, 6, left, lat + 1),
            copy(corner_east, west.at[:, low, :], 7, 7, right, lat + 1),
        )

    def folded():
        return copy(to_north, north, 5, 2, across, lat)

    def folded_east():
        return copy(corner_east, east.at[:, high, :], 6, 3, across_east, lat)

    def folded_west():
        return copy(corner_west, west.at[:, high, :], 7, 4, across_west, lat)

    def kept_east():
        return pltpu.make_async_copy(corner_east, east.at[:, high, :], keep_sem.at[0])

    def kept_west():
        return pltpu.make_async_copy(corner_west, west.at[:, high, :], keep_sem.at[1])

    @pl.when(has_south)
    def _():
        for c in southward():
            c.start()

    @pl.when(jnp.logical_not(northmost))
    def _():
        for c in northward():
            c.start()

    @pl.when(northmost)
    def _():
        folded().start()

        @pl.when(across_east != lon)
        def _():
            folded_east().start()

        @pl.when(across_east == lon)
        def _():
            kept_east().start()

        @pl.when(across_west != lon)
        def _():
            folded_west().start()

        @pl.when(across_west == lon)
        def _():
            kept_west().start()

    westward().start()
    eastward().start()

    @pl.when(jnp.logical_not(has_south))
    def _():
        south[...] = jnp.zeros(south.shape, jnp.float32)
        west[:, 0:HALO, :] = jnp.zeros((GROUPS, HALO, LANE), jnp.float32)
        east[:, 0:HALO, :] = jnp.zeros((GROUPS, HALO, LANE), jnp.float32)

    westward().wait()
    eastward().wait()

    @pl.when(has_south)
    def _():
        for c in southward():
            c.wait_send()
        for c in northward():
            c.wait_recv()

    @pl.when(jnp.logical_not(northmost))
    def _():
        for c in northward():
            c.wait_send()
        for c in southward():
            c.wait_recv()

    @pl.when(northmost)
    def _():
        folded().wait()

        @pl.when(across_east != lon)
        def _():
            folded_east().wait()

        @pl.when(across_east == lon)
        def _():
            kept_east().wait()

        @pl.when(across_west != lon)
        def _():
            folded_west().wait()

        @pl.when(across_west == lon)
        def _():
            kept_west().wait()


def exact_dot(x, selection):
    high, mid, low = split3(x)

    def dot(a):
        return jnp.dot(a, selection, preferred_element_type=jnp.float32)

    return (dot(high) + dot(mid)) + dot(low)


def substeps_kernel(
    lons, lats, state, mixing, land, north, south, west, east, out,
    natural, fixed, joined, first, second, mix, spin, fast, along, press, to_tiles, from_tiles, sems, out_sem,
):
    rows, cols = land.shape
    ext = rows + 2 * HALO
    depth = spin.shape[0]
    tiles = first.shape[2]
    lat = lax.axis_index("lat")
    middle = pl.ds(HALO, rows)

    loads = [
        c
        for t in range(cols // LANE)
        for c in (
            pltpu.make_async_copy(
                state.at[:, :, :, pl.ds(t * LANE, LANE)], natural.at[t, :, :, middle, :], sems.at[2 * t]
            ),
            pltpu.make_async_copy(
                mixing.at[:, :, pl.ds(t * LANE, LANE)],
                fixed.at[t, pl.ds(0, LEVELS), middle, :],
                sems.at[2 * t + 1],
            ),
        )
    ]
    for c in loads:
        c.start()

    def selection(shape, tile_dim):
        j = lax.broadcasted_iota(jnp.int32, shape, tile_dim)
        n = lax.broadcasted_iota(jnp.int32, shape, 1 - tile_dim)
        home = tiles * (j & (HALF - 1)) + j // HALF - HALO
        home = jnp.where(home < 0, home + tiles * HALF, home)
        return jnp.where((n == home) & (j < tiles * HALF), 1.0, 0.0).astype(jnp.bfloat16)

    to_tiles[...] = selection(to_tiles.shape, 1)
    from_tiles[...] = selection(from_tiles.shape, 0)

    r = lax.broadcasted_iota(jnp.int32, (depth, SUB, LANE), 0)
    s = lax.broadcasted_iota(jnp.int32, (depth, SUB, LANE), 1)
    h = lax.broadcasted_iota(jnp.int32, (depth, SUB, LANE), 2) // HALF
    total = rows * lats
    row = lat * rows - HALO + (SIDE * s + h) * depth + r
    row = jnp.where(row >= total, 2 * total - 1 - row, row).astype(jnp.float32)
    spin[...] = jnp.sin(jnp.pi * (row + 0.5) / total - jnp.pi / 2)

    for t in range(cols // LANE):
        span = slice(t * LANE, (t + 1) * LANE)
        for f in range(FIELDS):
            for k in range(LEVELS):
                natural[t, f, k, 0:HALO, :] = south[f * LEVELS + k, :, span]
                natural[t, f, k, ext - HALO : ext, :] = north[f * LEVELS + k, :, span]
        for p in range(LEVELS + 1):
            fixed[t, p, 0:HALO, :] = south[STATE + p, :, span]
            fixed[t, p, ext - HALO : ext, :] = north[STATE + p, :, span]
        fixed[t, LEVELS, HALO : HALO + rows, :] = land[:, span].astype(jnp.float32)
    for c in loads:
        c.wait()

    lane = lax.broadcasted_iota(jnp.int32, (SUB, LANE), 1)
    lower_half = lane < HALF
    west_at = tiles * HALF - cols - HALO

    def join(i, carry):
        for h in range(SIDE):
            picked = pl.ds(h * depth + i, SUB, stride=SIDE * depth)
            for g in range(GROUPS):
                e_all, w_all = east[g, picked, :], west[g, picked, :]
                for slot in range(PER_TILE):
                    p = g * PER_TILE + slot
                    e, w = e_all, w_all
                    if slot:
                        e = pltpu.roll(e, LANE - slot * HALO, 1)
                    if (west_at - slot * HALO) % LANE:
                        w = pltpu.roll(w, (west_at - slot * HALO) % LANE, 1)
                    side = jnp.where(
                        lane < HALO, e, jnp.where((lane >= west_at) & (lane < west_at + HALO), w, 0.0)
                    )
                    for t in range(cols // LANE):
                        if p < STATE:
                            value = natural[t, p // LEVELS, p % LEVELS, picked, :]
                        else:
                            value = fixed[t, p - STATE, picked, :]
                        joined[p, h, i, :, t * LANE : (t + 1) * LANE] = value
                    joined[p, h, i, :, cols : cols + LANE] = side
        return carry

    lax.fori_loop(0, depth, join, 0)

    half_rows = depth * SUB
    wide = cols + LANE
    low_lanes = lax.broadcasted_iota(jnp.int32, (half_rows, LANE), 1) < HALF

    def tiled(p):
        halves = []
        for h in range(SIDE):
            halves.append(exact_dot(joined[p, h].reshape(half_rows, wide), to_tiles[...]))
        result = []
        for c in range(tiles):
            span = slice(c // 2 * LANE, (c // 2 + 1) * LANE)
            a, b = halves[0][:, span], halves[1][:, span]
            if c % 2:
                a = pltpu.roll(a, HALF, 1)
            else:
                b = pltpu.roll(b, HALF, 1)
            result.append(jnp.where(low_lanes, a, b).reshape(depth, SUB, LANE))
        return result

    def place(p, carry):
        for c, value in enumerate(tiled(p)):
            first[p, 2 : depth + 2, c] = value
        return carry

    lax.fori_loop(0, STATE, place, 0)

    def place_fixed(p, carry):
        for c, value in enumerate(tiled(STATE + p)):
            mix[p, :, c] = value
        return carry

    lax.fori_loop(0, LEVELS + 1, place_fixed, 0)

    def ghosts(buf):
        def one(p, carry):
            for c in range(tiles):
                for to, source, ahead in ((0, depth, 0), (1, depth + 1, 0), (depth + 2, 2, 1), (depth + 3, 3, 1)):
                    x = pltpu.roll(buf[p, source, c], HALF, 1)
                    if ahead:
                        buf[p, to, c] = jnp.where(lower_half, x, pltpu.roll(x, SUB - 1, 0))
                    else:
                        buf[p, to, c] = jnp.where(lower_half, pltpu.roll(x, 1, 0), x)
            return carry

        lax.fori_loop(0, STATE, one, 0)

    def back(x):
        return pltpu.roll(x, 1, 1)

    def ahead(x):
        return pltpu.roll(x, LANE - 1, 1)

    def face(before, a, b, after):
        return 7.0 * (a + b) - (before + after)

    def prepare(q):
        def weights(j, carry):
            for c in range(tiles):
                running = None
                for k in range(LEVELS):
                    density = (
                        (-THERMAL * 0.5 * GRAVITY) * q[k, j + 1, c]
                        + (HALINE * 0.5 * GRAVITY) * q[LEVELS + k, j + 1, c]
                    )
                    running = density if running is None else running + density
                    press[k, j, c] = running
            return carry

        lax.fori_loop(0, depth + 2, weights, 0)

        def speeds(j, carry):
            for k in range(LEVELS):
                for c in range(tiles):
                    v = 3 * LEVELS + k
                    fast[k, j, c] = (q[v, j + 1, c] + q[v, j + 2, c]) * (1.0 / 24.0)
                u = [q[2 * LEVELS + k, j + 1, c] for c in range(tiles)]
                u.append(ahead(u[0]))
                for c in range(tiles):
                    along[k, j, c] = (u[c] + u[c + 1]) * (1.0 / 24.0)
            return carry

        lax.fori_loop(0, depth + 1, speeds, 0)

    chunk = depth // 2
    each = range(tiles)

    def advance(q, new):
        def rows_of(i, carry):
            base = i * chunk
            for k in range(LEVELS):
                for f in range(FIELDS):
                    p = f * LEVELS + k

                    def line(j, p=p):
                        return [q[p, base + j + 2, c] for c in each]

                    lines = {j: line(j) for j in (-2, -1, 0)}
                    lower = None
                    for j in range(-1, chunk):
                        lines[j + 2] = line(j + 2)
                        prev, here, succ, succ2 = (lines[j + d] for d in (-1, 0, 1, 2))
                        upper = [
                            fast[k, base + j + 1, c] * face(prev[c], here[c], succ[c], succ2[c]) for c in each
                        ]
                        if j < 0:
                            lower = upper
                            continue
                        ring = [back(here[-1])] + here + [ahead(here[0]), ahead(here[1])]
                        flux = [
                            along[k, base + j + 1, c] * face(ring[c], ring[c + 1], ring[c + 2], ring[c + 3])
                            for c in each
                        ]
                        flux = [back(flux[-1])] + flux
                        if f == 2:
                            load = [press[k, base + j + 1, c] for c in each]
                            load = [back(load[-1])] + load + [ahead(load[0])]
                        for c in each:
                            center = here[c]
                            advection = (flux[c + 1] - flux[c]) + (upper[c] - lower[c])
                            around = (ring[c] + ring[c + 2]) + (prev[c] + succ[c])
                            if f < 2:
                                if k == 0 or k == LEVELS - 1:
                                    other = q[p + (1 if k == 0 else -1), base + j + 2, c]
                                    mixed = around + (0.5 * other - 4.5 * center)
                                else:
                                    others = q[p - 1, base + j + 2, c] + q[p + 1, base + j + 2, c]
                                    mixed = around + (0.5 * others - 5.0 * center)
                            else:
                                mixed = around - 4.0 * center
                            tendency = mix[k, base + j, c] * mixed - advection
                            if f == 2:
                                turned = spin[base + j] * q[p + LEVELS, base + j + 2, c]
                                tendency = tendency + (turned - (load[c + 2] - load[c]))
                            elif f == 3:
                                turned = spin[base + j] * q[p - LEVELS, base + j + 2, c]
                                slope = press[k, base + j + 2, c] - press[k, base + j, c]
                                tendency = tendency - (turned + slope)
                            wet = TIMESTEP * mix[LEVELS, base + j, c]
                            new[p, base + j + 2, c] = center + wet * tendency
                        lower = upper
            return carry

        lax.fori_loop(0, depth // chunk, rows_of, 0)

    def pair(i, carry):
        for q, new in ((first, second), (second, first)):
            ghosts(q)
            prepare(q)
            advance(q, new)
        return carry

    lax.fori_loop(0, STEPS // 2, pair, 0)

    def gather(p, carry):
        value = [first[p, 2 : depth + 2, c].reshape(half_rows, LANE) for c in each]
        for h in range(SIDE):
            parts = []
            for c in range(0, tiles, 2):
                a = value[c] if h == 0 else pltpu.roll(value[c], HALF, 1)
                if c + 1 < tiles:
                    b = value[c + 1] if h == 1 else pltpu.roll(value[c + 1], HALF, 1)
                else:
                    b = jnp.zeros_like(a)
                parts.append(jnp.where(low_lanes, a, b))
            flat = exact_dot(jnp.concatenate(parts, axis=1), from_tiles[...])
            for i in range(depth):
                for t in range(cols // LANE):
                    natural[t, p // LEVELS, p % LEVELS, pl.ds(h * depth + i, SUB, stride=SIDE * depth), :] = flat[
                        i * SUB : (i + 1) * SUB, t * LANE : (t + 1) * LANE
                    ]
        return carry

    lax.fori_loop(0, STATE, gather, 0)
    stores = [
        pltpu.make_async_copy(
            natural.at[t, :, :, middle, :], out.at[:, :, :, pl.ds(t * LANE, LANE)], out_sem.at[t]
        )
        for t in range(cols // LANE)
    ]
    for c in stores:
        c.start()
    for c in stores:
        c.wait()


def body(lons, lats, ocean_state, mixing, land_sea):
    rows, cols = land_sea.shape
    ext, wide = rows + 2 * HALO, cols + LANE
    depth = ext // (SUB * SIDE)
    tiles = -(-(cols + 2 * HALO) // HALF)
    f32 = jnp.float32
    vmem = pl.BlockSpec(memory_space=pltpu.VMEM)
    hbm = pl.BlockSpec(memory_space=pl.ANY)
    halos = pl.pallas_call(
        functools.partial(exchange_kernel, lons, lats),
        out_shape=[
            jax.ShapeDtypeStruct((PLANES, HALO, cols), f32),
            jax.ShapeDtypeStruct((PLANES, HALO, cols), f32),
            jax.ShapeDtypeStruct((GROUPS, ext, LANE), f32),
            jax.ShapeDtypeStruct((GROUPS, ext, LANE), f32),
        ],
        in_specs=[vmem] * 3,
        out_specs=[vmem] * 4,
        scratch_shapes=[
            pltpu.VMEM((GROUPS, rows, LANE), f32),
            pltpu.VMEM((GROUPS, rows, LANE), f32),
            pltpu.VMEM((PLANES, HALO, cols), f32),
            pltpu.VMEM((PLANES, HALO, cols), f32),
            pltpu.VMEM((GROUPS, HALO, LANE), f32),
            pltpu.VMEM((GROUPS, HALO, LANE), f32),
            pltpu.SemaphoreType.DMA((8,)),
            pltpu.SemaphoreType.DMA((8,)),
            pltpu.SemaphoreType.DMA((2,)),
        ],
        compiler_params=pltpu.CompilerParams(
            collective_id=0, has_side_effects=True, vmem_limit_bytes=32 * 2**20
        ),
        name="exchange",
    )(ocean_state, mixing, land_sea)
    return pl.pallas_call(
        functools.partial(substeps_kernel, lons, lats),
        out_shape=jax.ShapeDtypeStruct(ocean_state.shape, f32),
        in_specs=[hbm, hbm] + [vmem] * 5,
        out_specs=hbm,
        scratch_shapes=[
            pltpu.VMEM((cols // LANE, FIELDS, LEVELS, ext, LANE), f32),
            pltpu.VMEM((cols // LANE, LEVELS + 1, ext, LANE), f32),
            pltpu.VMEM((PLANES, SIDE, depth, SUB, wide), f32),
            pltpu.VMEM((STATE, depth + 4, tiles, SUB, LANE), f32),
            pltpu.VMEM((STATE, depth + 4, tiles, SUB, LANE), f32),
            pltpu.VMEM((LEVELS + 1, depth, tiles, SUB, LANE), f32),
            pltpu.VMEM((depth, SUB, LANE), f32),
            pltpu.VMEM((LEVELS, depth + 1, tiles, SUB, LANE), f32),
            pltpu.VMEM((LEVELS, depth + 1, tiles, SUB, LANE), f32),
            pltpu.VMEM((LEVELS, depth + 2, tiles, SUB, LANE), f32),
            pltpu.VMEM((wide, wide), jnp.bfloat16),
            pltpu.VMEM((wide, cols), jnp.bfloat16),
            pltpu.SemaphoreType.DMA((2 * (cols // LANE),)),
            pltpu.SemaphoreType.DMA((cols // LANE,)),
        ],
        compiler_params=pltpu.CompilerParams(vmem_limit_bytes=48 * 2**20),
        name="substeps",
    )(ocean_state, mixing, land_sea, *halos)


def solution(mesh):
    in_specs = (P(None, None, "lat", "lon"), P(None, "lat", "lon"), P("lat", "lon"))
    out_specs = P(None, None, "lat", "lon")
    run = functools.partial(body, mesh.shape["lon"], mesh.shape["lat"])
    return jax.shard_map(run, mesh=mesh, in_specs=in_specs, out_specs=out_specs, check_vma=False)
```

```python
import functools

import jax
import jax.numpy as jnp
from jax import lax
from jax.experimental import pallas as pl
from jax.experimental.pallas import tpu as pltpu
from jax.sharding import PartitionSpec as P

STEPS = 8
HALO = 2 * STEPS
FIELDS = 4
LEVELS = 3
STATE = FIELDS * LEVELS
PLANES = STATE + LEVELS + 1
SUB = 8
LANE = 128
PER_TILE = LANE // HALO
GROUPS = PLANES // PER_TILE
SIDE = 2
HALF = LANE // SIDE

THERMAL = 0.2
HALINE = 0.15
GRAVITY = 0.5
TIMESTEP = 0.1


def split3(x):
    high = x.astype(jnp.bfloat16)
    rest = x - high.astype(jnp.float32)
    mid = rest.astype(jnp.bfloat16)
    low = (rest - mid.astype(jnp.float32)).astype(jnp.bfloat16)
    return high, mid, low


def flipped(block):
    x, span = block
    rows, cols = x.shape

    def reversal(size, group):
        i = lax.broadcasted_iota(jnp.int32, (size, size), 0)
        j = lax.broadcasted_iota(jnp.int32, (size, size), 1)
        partner = (i // group) * group + (group - 1 - i % group)
        return jnp.where(j == partner, 1.0, 0.0).astype(jnp.bfloat16)

    def dot(a, b):
        return jnp.dot(a, b, preferred_element_type=jnp.float32)

    flip_lanes = reversal(cols, span)
    flip_rows = reversal(rows, HALO)
    high, mid, low = split3(x)
    x = (dot(high, flip_lanes) + dot(mid, flip_lanes)) + dot(low, flip_lanes)
    high, mid, low = split3(x)
    return (dot(flip_rows, high) + dot(flip_rows, mid)) + dot(flip_rows, low)


def exchange_kernel(
    lons, lats, state, mixing, land, north, south, west, east,
    to_west, to_east, to_north, to_south, corner_west, corner_east, send_sem, recv_sem, keep_sem,
):
    rows, cols = land.shape
    ext = rows + 2 * HALO
    lon = lax.axis_index("lon")
    lat = lax.axis_index("lat")
    northmost = lat == lats - 1
    has_south = lat > 0
    left = lax.rem(lon + lons - 1, lons)
    right = lax.rem(lon + 1, lons)
    across = lons - 1 - lon
    across_east = lax.rem(2 * lons - 2 - lon, lons)
    across_west = lax.rem(lons - lon, lons)

    barrier = pltpu.get_barrier_semaphore()

    def greet(x, y):
        pl.semaphore_signal(barrier, inc=1, device_id=(x, y), device_id_type=pl.DeviceIdType.MESH)

    greet(left, lat)
    greet(right, lat)

    @pl.when(has_south)
    def _():
        for x in (left, lon, right):
            greet(x, lat - 1)

    @pl.when(jnp.logical_not(northmost))
    def _():
        for x in (left, lon, right):
            greet(x, lat + 1)

    @pl.when(northmost)
    def _():
        greet(across, lat)

        @pl.when(across_east != lon)
        def _():
            greet(across_east, lat)

        @pl.when(across_west != lon)
        def _():
            greet(across_west, lat)

    def plane(p, row_slice, col_slice):
        if p < STATE:
            return state[p // LEVELS, p % LEVELS, row_slice, col_slice]
        if p < STATE + LEVELS:
            return mixing[p - STATE, row_slice, col_slice]
        return land[row_slice, col_slice].astype(jnp.float32)

    everything = slice(0, cols)
    for p in range(PLANES):
        to_south[p] = plane(p, slice(0, HALO), everything)
        to_north[p] = plane(p, slice(rows - HALO, rows), everything)

    lane = lax.broadcasted_iota(jnp.int32, (rows, LANE), 1)
    for g in range(GROUPS):
        packed_west = jnp.zeros((rows, LANE), jnp.float32)
        packed_east = jnp.zeros((rows, LANE), jnp.float32)
        for slot in range(PER_TILE):
            p = g * PER_TILE + slot
            here = (lane >= slot * HALO) & (lane < (slot + 1) * HALO)
            first = plane(p, slice(0, rows), slice(0, LANE))
            last = plane(p, slice(0, rows), slice(cols - LANE, cols))
            if slot:
                first = pltpu.roll(first, slot * HALO, 1)
            if (slot + 1) * HALO != LANE:
                last = pltpu.roll(last, (slot + 1) * HALO, 1)
            packed_west = jnp.where(here, first, packed_west)
            packed_east = jnp.where(here, last, packed_east)
        to_west[g] = packed_west
        to_east[g] = packed_east

    @pl.when(northmost)
    def _():
        full = to_north[...].reshape(PLANES * HALO, cols)
        index = lax.broadcasted_iota(jnp.int32, full.shape, 0) // HALO
        odd = (index >= 2 * LEVELS) & (index < STATE)
        full = flipped((full, cols))
        to_north[...] = jnp.where(odd, -full, full).reshape(PLANES, HALO, cols)
        shape = (GROUPS * HALO, LANE)
        index = (
            lax.broadcasted_iota(jnp.int32, shape, 0) // HALO * PER_TILE
            + lax.broadcasted_iota(jnp.int32, shape, 1) // HALO
        )
        odd = (index >= 2 * LEVELS) & (index < STATE)
        for source, corner in ((to_west, corner_west), (to_east, corner_east)):
            strip = flipped((source[:, rows - HALO :, :].reshape(shape), HALO))
            corner[...] = jnp.where(odd, -strip, strip).reshape(GROUPS, HALO, LANE)

    @pl.when(jnp.logical_not(northmost))
    def _():
        corner_west[...] = to_west[:, rows - HALO :, :]
        corner_east[...] = to_east[:, rows - HALO :, :]

    @pl.when(has_south & jnp.logical_not(northmost))
    def _():
        pl.semaphore_wait(barrier, 8)

    @pl.when(jnp.logical_not(has_south) & jnp.logical_not(northmost))
    def _():
        pl.semaphore_wait(barrier, 5)

    @pl.when(northmost)
    def _():
        folds = (
            1
            + (across_east != lon).astype(jnp.int32)
            + (across_west != lon).astype(jnp.int32)
        )
        pl.semaphore_wait(barrier, 2 + 3 * has_south.astype(jnp.int32) + folds)

    low = pl.ds(0, HALO)
    high = pl.ds(ext - HALO, HALO)
    middle = pl.ds(HALO, rows)

    def copy(src, dst, send, recv, x, y):
        return pltpu.make_async_remote_copy(
            src_ref=src,
            dst_ref=dst,
            send_sem=send_sem.at[send],
            recv_sem=recv_sem.at[recv],
            device_id=(x, y),
            device_id_type=pl.DeviceIdType.MESH,
        )

    def westward():
        return copy(to_west, east.at[:, middle, :], 0, 1, left, lat)

    def eastward():
        return copy(to_east, west.at[:, middle, :], 1, 0, right, lat)

    def southward():
        return (
            copy(to_south, north, 2, 2, lon, lat - 1),
            copy(to_west.at[:, low, :], east.at[:, high, :], 3, 3, left, lat - 1),
            copy(to_east.at[:, low, :], west.at[:, high, :], 4, 4, right, lat - 1),
        )

    def northward():
        return (
            copy(to_north, south, 5, 5, lon, lat + 1),
            copy(corner_west, east.at[:, low, :], 6, 6, left, lat + 1),
            copy(corner_east, west.at[:, low, :], 7, 7, right, lat + 1),
        )

    def folded():
        return copy(to_north, north, 5, 2, across, lat)

    def folded_east():
        return copy(corner_east, east.at[:, high, :], 6, 3, across_east, lat)

    def folded_west():
        return copy(corner_west, west.at[:, high, :], 7, 4, across_west, lat)

    def kept_east():
        return pltpu.make_async_copy(corner_east, east.at[:, high, :], keep_sem.at[0])

    def kept_west():
        return pltpu.make_async_copy(corner_west, west.at[:, high, :], keep_sem.at[1])

    @pl.when(has_south)
    def _():
        for c in southward():
            c.start()

    @pl.when(jnp.logical_not(northmost))
    def _():
        for c in northward():
            c.start()

    @pl.when(northmost)
    def _():
        folded().start()

        @pl.when(across_east != lon)
        def _():
            folded_east().start()

        @pl.when(across_east == lon)
        def _():
            kept_east().start()

        @pl.when(across_west != lon)
        def _():
            folded_west().start()

        @pl.when(across_west == lon)
        def _():
            kept_west().start()

    westward().start()
    eastward().start()

    @pl.when(jnp.logical_not(has_south))
    def _():
        south[...] = jnp.zeros(south.shape, jnp.float32)
        west[:, 0:HALO, :] = jnp.zeros((GROUPS, HALO, LANE), jnp.float32)
        east[:, 0:HALO, :] = jnp.zeros((GROUPS, HALO, LANE), jnp.float32)

    westward().wait()
    eastward().wait()

    @pl.when(has_south)
    def _():
        for c in southward():
            c.wait_send()
        for c in northward():
            c.wait_recv()

    @pl.when(jnp.logical_not(northmost))
    def _():
        for c in northward():
            c.wait_send()
        for c in southward():
            c.wait_recv()

    @pl.when(northmost)
    def _():
        folded().wait()

        @pl.when(across_east != lon)
        def _():
            folded_east().wait()

        @pl.when(across_east == lon)
        def _():
            kept_east().wait()

        @pl.when(across_west != lon)
        def _():
            folded_west().wait()

        @pl.when(across_west == lon)
        def _():
            kept_west().wait()


def exact_dot(x, selection):
    rows = x.shape[0]
    pieces = jnp.concatenate(split3(x), axis=0)
    y = jnp.dot(pieces, selection, preferred_element_type=jnp.float32)
    return (y[:rows] + y[rows : 2 * rows]) + y[2 * rows :]


def substeps_kernel(
    lons, lats, state, mixing, land, north, south, west, east, out,
    natural, fixed, joined, first, second, mix, spin, fast, along, press, to_tiles, from_tiles, sems, out_sem,
):
    rows, cols = land.shape
    ext = rows + 2 * HALO
    depth = spin.shape[0]
    tiles = mix.shape[2]
    lat = lax.axis_index("lat")
    middle = pl.ds(HALO, rows)

    loads = [
        c
        for t in range(cols // LANE)
        for c in (
            pltpu.make_async_copy(
                state.at[:, :, :, pl.ds(t * LANE, LANE)], natural.at[t, :, :, middle, :], sems.at[2 * t]
            ),
            pltpu.make_async_copy(
                mixing.at[:, :, pl.ds(t * LANE, LANE)],
                fixed.at[t, pl.ds(0, LEVELS), middle, :],
                sems.at[2 * t + 1],
            ),
        )
    ]
    for c in loads:
        c.start()

    def selection(shape, tile_dim):
        j = lax.broadcasted_iota(jnp.int32, shape, tile_dim)
        n = lax.broadcasted_iota(jnp.int32, shape, 1 - tile_dim)
        home = tiles * (j & (HALF - 1)) + j // HALF - HALO
        home = jnp.where(home < 0, home + tiles * HALF, home)
        return jnp.where((n == home) & (j < tiles * HALF), 1.0, 0.0).astype(jnp.bfloat16)

    to_tiles[...] = selection(to_tiles.shape, 1)
    from_tiles[...] = selection(from_tiles.shape, 0)

    r = lax.broadcasted_iota(jnp.int32, (depth, SUB, LANE), 0)
    s = lax.broadcasted_iota(jnp.int32, (depth, SUB, LANE), 1)
    h = lax.broadcasted_iota(jnp.int32, (depth, SUB, LANE), 2) // HALF
    total = rows * lats
    row = lat * rows - HALO + (SIDE * s + h) * depth + r
    row = jnp.where(row >= total, 2 * total - 1 - row, row).astype(jnp.float32)
    spin[...] = jnp.sin(jnp.pi * (row + 0.5) / total - jnp.pi / 2)

    for t in range(cols // LANE):
        span = slice(t * LANE, (t + 1) * LANE)
        for f in range(FIELDS):
            for k in range(LEVELS):
                natural[t, f, k, 0:HALO, :] = south[f * LEVELS + k, :, span]
                natural[t, f, k, ext - HALO : ext, :] = north[f * LEVELS + k, :, span]
        for p in range(LEVELS + 1):
            fixed[t, p, 0:HALO, :] = south[STATE + p, :, span]
            fixed[t, p, ext - HALO : ext, :] = north[STATE + p, :, span]
        fixed[t, LEVELS, HALO : HALO + rows, :] = land[:, span].astype(jnp.float32)
    for c in loads:
        c.wait()

    lane = lax.broadcasted_iota(jnp.int32, (SUB, LANE), 1)
    lower_half = lane < HALF
    west_at = tiles * HALF - cols - HALO

    def join(i, carry):
        for h in range(SIDE):
            picked = pl.ds(h * depth + i, SUB, stride=SIDE * depth)
            for g in range(GROUPS):
                e_all, w_all = east[g, picked, :], west[g, picked, :]
                for slot in range(PER_TILE):
                    p = g * PER_TILE + slot
                    e, w = e_all, w_all
                    if slot:
                        e = pltpu.roll(e, LANE - slot * HALO, 1)
                    if (west_at - slot * HALO) % LANE:
                        w = pltpu.roll(w, (west_at - slot * HALO) % LANE, 1)
                    side = jnp.where(
                        lane < HALO, e, jnp.where((lane >= west_at) & (lane < west_at + HALO), w, 0.0)
                    )
                    for t in range(cols // LANE):
                        if p < STATE:
                            value = natural[t, p // LEVELS, p % LEVELS, picked, :]
                        else:
                            value = fixed[t, p - STATE, picked, :]
                        joined[p, h, i, :, t * LANE : (t + 1) * LANE] = value
                    joined[p, h, i, :, cols : cols + LANE] = side
        return carry

    lax.fori_loop(0, depth, join, 0)

    half_rows = depth * SUB
    wide = cols + LANE
    low_lanes = lax.broadcasted_iota(jnp.int32, (half_rows, LANE), 1) < HALF

    each = range(tiles)
    edge = 2

    def back(x):
        return pltpu.roll(x, 1, 1)

    def ahead(x):
        return pltpu.roll(x, LANE - 1, 1)

    def publish(buf, p, j, row):
        for c in each:
            buf[p, j + 2, c + edge] = row[c]
        buf[p, j + 2, 0] = back(row[-2])
        buf[p, j + 2, 1] = back(row[-1])
        buf[p, j + 2, tiles + edge] = ahead(row[0])
        buf[p, j + 2, tiles + edge + 1] = ahead(row[1])
        if j < 2:
            for c in each:
                x = pltpu.roll(row[c], HALF, 1)
                buf[p, depth + 2 + j, c + edge] = jnp.where(lower_half, x, pltpu.roll(x, SUB - 1, 0))
        if j >= depth - 2:
            for c in each:
                x = pltpu.roll(row[c], HALF, 1)
                buf[p, j + 2 - depth, c + edge] = jnp.where(lower_half, pltpu.roll(x, 1, 0), x)

    def tiled(p):
        both = exact_dot(joined[p].reshape(SIDE * half_rows, wide), to_tiles[...])
        result = []
        for c in each:
            span = slice(c // 2 * LANE, (c // 2 + 1) * LANE)
            a, b = both[:half_rows, span], both[half_rows:, span]
            if c % 2:
                a = pltpu.roll(a, HALF, 1)
            else:
                b = pltpu.roll(b, HALF, 1)
            result.append(jnp.where(low_lanes, a, b))
        return result

    def place(p, carry):
        values = tiled(p)
        for j in range(depth):
            publish(first, p, j, [x[j * SUB : (j + 1) * SUB] for x in values])
        return carry

    lax.fori_loop(0, STATE, place, 0)

    def place_fixed(p, carry):
        for c, value in enumerate(tiled(STATE + p)):
            mix[p, :, c] = value.reshape(depth, SUB, LANE)
        return carry

    lax.fori_loop(0, LEVELS + 1, place_fixed, 0)
    mix[LEVELS] = TIMESTEP * mix[LEVELS]

    def face(before, a, b, after):
        return 7.0 * (a + b) - (before + after)

    def weigh(q):
        for j in range(-1, depth + 1):
            beside = 1 if 0 <= j < depth else 0
            for c in range(-beside, tiles + beside):
                running = None
                for k in range(LEVELS):
                    density = (
                        (-THERMAL * 0.5 * GRAVITY) * q[k, j + 2, c + edge]
                        + (HALINE * 0.5 * GRAVITY) * q[LEVELS + k, j + 2, c + edge]
                    )
                    running = density if running is None else running + density
                    press[k, j + 1, c + 1] = running

    def advance(q, new):
        weigh(q)

        def level(k, carry):
            zonal, merid = 2 * LEVELS + k, 3 * LEVELS + k
            above, under = jnp.maximum(k - 1, 0), jnp.minimum(k + 1, LEVELS - 1)
            for j in range(depth + 1):
                for c in each:
                    fast[j, c] = (q[merid, j + 1, c + edge] + q[merid, j + 2, c + edge]) * (1.0 / 24.0)
            for j in range(depth):
                for c in range(tiles + 1):
                    along[j, c] = (q[zonal, j + 2, c + 1] + q[zonal, j + 2, c + 2]) * (1.0 / 24.0)
            for f in range(FIELDS):
                p = f * LEVELS + k

                def line(j, p=p):
                    return [q[p, j + 2, c + edge] for c in each]

                lines = {j: line(j) for j in (-2, -1, 0)}
                lower = None
                for j in range(-1, depth):
                    lines[j + 2] = line(j + 2)
                    prev, here, succ, succ2 = (lines[j + d] for d in (-1, 0, 1, 2))
                    upper = [fast[j + 1, c] * face(prev[c], here[c], succ[c], succ2[c]) for c in each]
                    if j < 0:
                        lower = upper
                        continue
                    ring = (
                        [q[p, j + 2, 0], q[p, j + 2, 1]]
                        + here
                        + [q[p, j + 2, tiles + edge], q[p, j + 2, tiles + edge + 1]]
                    )
                    flux = [
                        along[j, c] * face(ring[c], ring[c + 1], ring[c + 2], ring[c + 3])
                        for c in range(tiles + 1)
                    ]
                    row = []
                    for c in each:
                        center = here[c]
                        advection = (flux[c + 1] - flux[c]) + (upper[c] - lower[c])
                        around = (ring[c + 1] + ring[c + 3]) + (prev[c] + succ[c])
                        if f < 2:
                            others = q[f * LEVELS + above, j + 2, c + edge] + q[f * LEVELS + under, j + 2, c + edge]
                            mixed = around + (0.5 * others - 5.0 * center)
                        else:
                            mixed = around - 4.0 * center
                        tendency = mix[k, j, c] * mixed - advection
                        if f == 2:
                            slope = press[k, j + 1, c + 2] - press[k, j + 1, c]
                            tendency = tendency + (spin[j] * q[merid, j + 2, c + edge] - slope)
                        elif f == 3:
                            slope = press[k, j + 2, c + 1] - press[k, j, c + 1]
                            tendency = tendency - (spin[j] * q[zonal, j + 2, c + edge] + slope)
                        row.append(center + mix[LEVELS, j, c] * tendency)
                    publish(new, p, j, row)
                    lower = upper
            return carry

        lax.fori_loop(0, LEVELS, level, 0)

    def pair(i, carry):
        advance(first, second)
        advance(second, first)
        return carry

    lax.fori_loop(0, STEPS // 2, pair, 0)

    def gather(p, carry):
        value = [first[p, 2 : depth + 2, c + edge].reshape(half_rows, LANE) for c in each]
        halves = []
        for h in range(SIDE):
            parts = []
            for c in range(0, tiles, 2):
                a = value[c] if h == 0 else pltpu.roll(value[c], HALF, 1)
                if c + 1 < tiles:
                    b = value[c + 1] if h == 1 else pltpu.roll(value[c + 1], HALF, 1)
                else:
                    b = jnp.zeros_like(a)
                parts.append(jnp.where(low_lanes, a, b))
            halves.append(jnp.concatenate(parts, axis=1))
        flat = exact_dot(jnp.concatenate(halves, axis=0), from_tiles[...])
        for h in range(SIDE):
            for i in range(depth):
                at = (h * depth + i) * SUB
                for t in range(cols // LANE):
                    natural[t, p // LEVELS, p % LEVELS, pl.ds(h * depth + i, SUB, stride=SIDE * depth), :] = flat[
                        at : at + SUB, t * LANE : (t + 1) * LANE
                    ]
        return carry

    lax.fori_loop(0, STATE, gather, 0)
    stores = [
        pltpu.make_async_copy(
            natural.at[t, :, :, middle, :], out.at[:, :, :, pl.ds(t * LANE, LANE)], out_sem.at[t]
        )
        for t in range(cols // LANE)
    ]
    for c in stores:
        c.start()
    for c in stores:
        c.wait()


def body(lons, lats, ocean_state, mixing, land_sea):
    rows, cols = land_sea.shape
    ext, wide = rows + 2 * HALO, cols + LANE
    depth = ext // (SUB * SIDE)
    tiles = -(-(cols + 2 * HALO) // HALF)
    f32 = jnp.float32
    vmem = pl.BlockSpec(memory_space=pltpu.VMEM)
    hbm = pl.BlockSpec(memory_space=pl.ANY)
    halos = pl.pallas_call(
        functools.partial(exchange_kernel, lons, lats),
        out_shape=[
            jax.ShapeDtypeStruct((PLANES, HALO, cols), f32),
            jax.ShapeDtypeStruct((PLANES, HALO, cols), f32),
            jax.ShapeDtypeStruct((GROUPS, ext, LANE), f32),
            jax.ShapeDtypeStruct((GROUPS, ext, LANE), f32),
        ],
        in_specs=[vmem] * 3,
        out_specs=[vmem] * 4,
        scratch_shapes=[
            pltpu.VMEM((GROUPS, rows, LANE), f32),
            pltpu.VMEM((GROUPS, rows, LANE), f32),
            pltpu.VMEM((PLANES, HALO, cols), f32),
            pltpu.VMEM((PLANES, HALO, cols), f32),
            pltpu.VMEM((GROUPS, HALO, LANE), f32),
            pltpu.VMEM((GROUPS, HALO, LANE), f32),
            pltpu.SemaphoreType.DMA((8,)),
            pltpu.SemaphoreType.DMA((8,)),
            pltpu.SemaphoreType.DMA((2,)),
        ],
        compiler_params=pltpu.CompilerParams(
            collective_id=0, has_side_effects=True, vmem_limit_bytes=32 * 2**20
        ),
        name="exchange",
    )(ocean_state, mixing, land_sea)
    return pl.pallas_call(
        functools.partial(substeps_kernel, lons, lats),
        out_shape=jax.ShapeDtypeStruct(ocean_state.shape, f32),
        in_specs=[hbm, hbm] + [vmem] * 5,
        out_specs=hbm,
        scratch_shapes=[
            pltpu.VMEM((cols // LANE, FIELDS, LEVELS, ext, LANE), f32),
            pltpu.VMEM((cols // LANE, LEVELS + 1, ext, LANE), f32),
            pltpu.VMEM((PLANES, SIDE, depth, SUB, wide), f32),
            pltpu.VMEM((STATE, depth + 4, tiles + 4, SUB, LANE), f32),
            pltpu.VMEM((STATE, depth + 4, tiles + 4, SUB, LANE), f32),
            pltpu.VMEM((LEVELS + 1, depth, tiles, SUB, LANE), f32),
            pltpu.VMEM((depth, SUB, LANE), f32),
            pltpu.VMEM((depth + 1, tiles, SUB, LANE), f32),
            pltpu.VMEM((depth, tiles + 1, SUB, LANE), f32),
            pltpu.VMEM((LEVELS, depth + 2, tiles + 2, SUB, LANE), f32),
            pltpu.VMEM((wide, wide), jnp.bfloat16),
            pltpu.VMEM((wide, cols), jnp.bfloat16),
            pltpu.SemaphoreType.DMA((2 * (cols // LANE),)),
            pltpu.SemaphoreType.DMA((cols // LANE,)),
        ],
        compiler_params=pltpu.CompilerParams(vmem_limit_bytes=48 * 2**20),
        name="substeps",
    )(ocean_state, mixing, land_sea, *halos)


def solution(mesh):
    in_specs = (P(None, None, "lat", "lon"), P(None, "lat", "lon"), P("lat", "lon"))
    out_specs = P(None, None, "lat", "lon")
    run = functools.partial(body, mesh.shape["lon"], mesh.shape["lat"])
    return jax.shard_map(run, mesh=mesh, in_specs=in_specs, out_specs=out_specs, check_vma=False)
```

```python
import functools

import jax
import jax.numpy as jnp
from jax import lax
from jax.experimental import pallas as pl
from jax.experimental.pallas import tpu as pltpu
from jax.sharding import PartitionSpec as P

STEPS = 8
HALO = 2 * STEPS
FIELDS = 4
LEVELS = 3
STATE = FIELDS * LEVELS
PLANES = STATE + LEVELS + 1
SUB = 8
LANE = 128
PER_TILE = LANE // HALO
GROUPS = PLANES // PER_TILE
SIDE = 2
HALF = LANE // SIDE

THERMAL = 0.2
HALINE = 0.15
GRAVITY = 0.5
TIMESTEP = 0.1


def split3(x):
    high = x.astype(jnp.bfloat16)
    rest = x - high.astype(jnp.float32)
    mid = rest.astype(jnp.bfloat16)
    low = (rest - mid.astype(jnp.float32)).astype(jnp.bfloat16)
    return high, mid, low


def flipped(block):
    x, span = block
    rows, cols = x.shape

    def reversal(size, group):
        i = lax.broadcasted_iota(jnp.int32, (size, size), 0)
        j = lax.broadcasted_iota(jnp.int32, (size, size), 1)
        return jnp.where(j == (i ^ (group - 1)), 1.0, 0.0).astype(jnp.bfloat16)

    def dot(a, b):
        return jnp.dot(a, b, preferred_element_type=jnp.float32)

    flip_lanes = reversal(cols, span)
    flip_rows = reversal(rows, HALO)
    high, mid, low = split3(x)
    x = (dot(high, flip_lanes) + dot(mid, flip_lanes)) + dot(low, flip_lanes)
    high, mid, low = split3(x)
    return (dot(flip_rows, high) + dot(flip_rows, mid)) + dot(flip_rows, low)


def exchange_kernel(
    lons, lats, state, mixing, land, natural, west, east, to_tiles, from_tiles, spin,
    to_west, to_east, to_north, corner_west, corner_east, land_here, send_sem, recv_sem, keep_sem, load_sem,
):
    rows, cols = land.shape
    ext = rows + 2 * HALO
    lon = lax.axis_index("lon")
    lat = lax.axis_index("lat")
    northmost = lat == lats - 1
    has_south = lat > 0
    left = lax.rem(lon + lons - 1, lons)
    right = lax.rem(lon + 1, lons)
    across = lons - 1 - lon
    across_east = lax.rem(2 * lons - 2 - lon, lons)
    across_west = lax.rem(lons - lon, lons)

    low = pl.ds(0, HALO)
    high = pl.ds(ext - HALO, HALO)
    middle = pl.ds(HALO, rows)
    lane_tiles = cols // LANE

    loads = [pltpu.make_async_copy(land, land_here, load_sem.at[0])]
    for t in range(lane_tiles):
        span = pl.ds(t * LANE, LANE)
        for f in range(FIELDS):
            loads.append(
                pltpu.make_async_copy(
                    state.at[f, :, :, span],
                    natural.at[t, pl.ds(f * LEVELS, LEVELS), middle, :],
                    load_sem.at[len(loads)],
                )
            )
        loads.append(
            pltpu.make_async_copy(
                mixing.at[:, :, span], natural.at[t, pl.ds(STATE, LEVELS), middle, :], load_sem.at[len(loads)]
            )
        )
    for c in loads:
        c.start()

    barrier = pltpu.get_barrier_semaphore()

    def greet(x, y):
        pl.semaphore_signal(barrier, inc=1, device_id=(x, y), device_id_type=pl.DeviceIdType.MESH)

    greet(left, lat)
    greet(right, lat)

    @pl.when(has_south)
    def _():
        for x in (left, lon, right):
            greet(x, lat - 1)

    @pl.when(jnp.logical_not(northmost))
    def _():
        for x in (left, lon, right):
            greet(x, lat + 1)

    @pl.when(northmost)
    def _():
        greet(across, lat)

        @pl.when(across_east != lon)
        def _():
            greet(across_east, lat)

        @pl.when(across_west != lon)
        def _():
            greet(across_west, lat)

    for c in loads:
        c.wait()
    for t in range(lane_tiles):
        natural[t, PLANES - 1, HALO : HALO + rows, :] = land_here[:, t * LANE : (t + 1) * LANE].astype(jnp.float32)

    lane = lax.broadcasted_iota(jnp.int32, (rows, LANE), 1)
    for g in range(GROUPS):
        packed_west = jnp.zeros((rows, LANE), jnp.float32)
        packed_east = jnp.zeros((rows, LANE), jnp.float32)
        for slot in range(PER_TILE):
            p = g * PER_TILE + slot
            here = (lane >= slot * HALO) & (lane < (slot + 1) * HALO)
            first = natural[0, p, HALO : HALO + rows, :]
            last = natural[lane_tiles - 1, p, HALO : HALO + rows, :]
            if slot:
                first = pltpu.roll(first, slot * HALO, 1)
            if (slot + 1) * HALO != LANE:
                last = pltpu.roll(last, (slot + 1) * HALO, 1)
            packed_west = jnp.where(here, first, packed_west)
            packed_east = jnp.where(here, last, packed_east)
        to_west[g] = packed_west
        to_east[g] = packed_east

    @pl.when(northmost)
    def _():
        top = [natural[t, :, rows : rows + HALO, :].reshape(PLANES * HALO, LANE) for t in range(lane_tiles)]
        full = jnp.concatenate(top, axis=1)
        index = lax.broadcasted_iota(jnp.int32, full.shape, 0) >> (HALO.bit_length() - 1)
        odd = (index >= 2 * LEVELS) & (index < STATE)
        full = flipped((full, cols))
        full = jnp.where(odd, -full, full)
        for t in range(lane_tiles):
            to_north[t] = full[:, t * LANE : (t + 1) * LANE].reshape(PLANES, HALO, LANE)
        shape = (GROUPS * HALO, LANE)
        index = (
            lax.broadcasted_iota(jnp.int32, shape, 0) // HALO * PER_TILE
            + lax.broadcasted_iota(jnp.int32, shape, 1) // HALO
        )
        odd = (index >= 2 * LEVELS) & (index < STATE)
        for source, corner in ((to_west, corner_west), (to_east, corner_east)):
            strip = flipped((source[:, rows - HALO :, :].reshape(shape), HALO))
            corner[...] = jnp.where(odd, -strip, strip).reshape(GROUPS, HALO, LANE)

    @pl.when(jnp.logical_not(northmost))
    def _():
        corner_west[...] = to_west[:, rows - HALO :, :]
        corner_east[...] = to_east[:, rows - HALO :, :]

    @pl.when(has_south & jnp.logical_not(northmost))
    def _():
        pl.semaphore_wait(barrier, 8)

    @pl.when(jnp.logical_not(has_south) & jnp.logical_not(northmost))
    def _():
        pl.semaphore_wait(barrier, 5)

    @pl.when(northmost)
    def _():
        folds = (
            1
            + (across_east != lon).astype(jnp.int32)
            + (across_west != lon).astype(jnp.int32)
        )
        pl.semaphore_wait(barrier, 2 + 3 * has_south.astype(jnp.int32) + folds)

    def copy(src, dst, send, recv, x, y):
        return pltpu.make_async_remote_copy(
            src_ref=src,
            dst_ref=dst,
            send_sem=send_sem.at[send],
            recv_sem=recv_sem.at[recv],
            device_id=(x, y),
            device_id_type=pl.DeviceIdType.MESH,
        )

    def westward():
        return copy(to_west, east.at[:, middle, :], 0, 1, left, lat)

    def eastward():
        return copy(to_east, west.at[:, middle, :], 1, 0, right, lat)

    def southward():
        return (
            copy(natural.at[:, :, pl.ds(HALO, HALO), :], natural.at[:, :, high, :], 2, 2, lon, lat - 1),
            copy(to_west.at[:, low, :], east.at[:, high, :], 3, 3, left, lat - 1),
            copy(to_east.at[:, low, :], west.at[:, high, :], 4, 4, right, lat - 1),
        )

    def northward():
        return (
            copy(natural.at[:, :, pl.ds(rows, HALO), :], natural.at[:, :, low, :], 5, 5, lon, lat + 1),
            copy(corner_west, east.at[:, low, :], 6, 6, left, lat + 1),
            copy(corner_east, west.at[:, low, :], 7, 7, right, lat + 1),
        )

    def folded():
        return copy(to_north, natural.at[:, :, high, :], 5, 2, across, lat)

    def folded_east():
        return copy(corner_east, east.at[:, high, :], 6, 3, across_east, lat)

    def folded_west():
        return copy(corner_west, west.at[:, high, :], 7, 4, across_west, lat)

    def kept_east():
        return pltpu.make_async_copy(corner_east, east.at[:, high, :], keep_sem.at[0])

    def kept_west():
        return pltpu.make_async_copy(corner_west, west.at[:, high, :], keep_sem.at[1])

    @pl.when(has_south)
    def _():
        for c in southward():
            c.start()

    @pl.when(jnp.logical_not(northmost))
    def _():
        for c in northward():
            c.start()

    @pl.when(northmost)
    def _():
        folded().start()

        @pl.when(across_east != lon)
        def _():
            folded_east().start()

        @pl.when(across_east == lon)
        def _():
            kept_east().start()

        @pl.when(across_west != lon)
        def _():
            folded_west().start()

        @pl.when(across_west == lon)
        def _():
            kept_west().start()

    westward().start()
    eastward().start()

    @pl.when(jnp.logical_not(has_south))
    def _():
        natural[:, :, 0:HALO, :] = jnp.zeros((lane_tiles, PLANES, HALO, LANE), jnp.float32)
        west[:, 0:HALO, :] = jnp.zeros((GROUPS, HALO, LANE), jnp.float32)
        east[:, 0:HALO, :] = jnp.zeros((GROUPS, HALO, LANE), jnp.float32)

    tiles = -(-(cols + 2 * HALO) // HALF)
    depth = spin.shape[0]
    def selection(shape, tile_dim):
        j = lax.broadcasted_iota(jnp.int32, shape, tile_dim)
        n = lax.broadcasted_iota(jnp.int32, shape, 1 - tile_dim)
        home = tiles * (j & (HALF - 1)) + (j >> (HALF.bit_length() - 1)) - HALO
        home = jnp.where(home < 0, home + tiles * HALF, home)
        return jnp.where((n == home) & (j < tiles * HALF), 1.0, 0.0).astype(jnp.bfloat16)

    to_tiles[...] = selection(to_tiles.shape, 1)
    from_tiles[...] = selection(from_tiles.shape, 0)

    r = lax.broadcasted_iota(jnp.int32, (depth, SUB, LANE), 0)
    s = lax.broadcasted_iota(jnp.int32, (depth, SUB, LANE), 1)
    h = lax.broadcasted_iota(jnp.int32, (depth, SUB, LANE), 2) >> (HALF.bit_length() - 1)
    total = rows * lats
    row = lat * rows - HALO + (SIDE * s + h) * depth + r
    row = jnp.where(row >= total, 2 * total - 1 - row, row).astype(jnp.float32)
    spin[...] = jnp.sin(jnp.pi * (row + 0.5) / total - jnp.pi / 2)

    westward().wait()
    eastward().wait()

    @pl.when(has_south)
    def _():
        for c in southward():
            c.wait_send()
        for c in northward():
            c.wait_recv()

    @pl.when(jnp.logical_not(northmost))
    def _():
        for c in northward():
            c.wait_send()
        for c in southward():
            c.wait_recv()

    @pl.when(northmost)
    def _():
        folded().wait()

        @pl.when(across_east != lon)
        def _():
            folded_east().wait()

        @pl.when(across_east == lon)
        def _():
            kept_east().wait()

        @pl.when(across_west != lon)
        def _():
            folded_west().wait()

        @pl.when(across_west == lon)
        def _():
            kept_west().wait()


def exact_dot(x, selection):
    rows = x.shape[0]
    pieces = jnp.concatenate(split3(x), axis=0)
    y = jnp.dot(pieces, selection, preferred_element_type=jnp.float32)
    return (y[:rows] + y[rows : 2 * rows]) + y[2 * rows :]


def substeps_kernel(
    natural, west, east, to_tiles, from_tiles, spin, out,
    joined, first, second, mix, fast, along, press, result, out_sem,
):
    lane_tiles, _, ext, _ = natural.shape
    rows, cols = ext - 2 * HALO, lane_tiles * LANE
    depth = spin.shape[0]
    tiles = mix.shape[2]
    middle = pl.ds(HALO, rows)

    lane = lax.broadcasted_iota(jnp.int32, (SUB, LANE), 1)
    lower_half = lane < HALF
    west_at = tiles * HALF - cols - HALO

    def join(i, carry):
        for h in range(SIDE):
            picked = pl.ds(h * depth + i, SUB, stride=SIDE * depth)
            for g in range(GROUPS):
                e_all, w_all = east[g, picked, :], west[g, picked, :]
                for slot in range(PER_TILE):
                    p = g * PER_TILE + slot
                    e, w = e_all, w_all
                    if slot:
                        e = pltpu.roll(e, LANE - slot * HALO, 1)
                    if (west_at - slot * HALO) % LANE:
                        w = pltpu.roll(w, (west_at - slot * HALO) % LANE, 1)
                    side = jnp.where(
                        lane < HALO, e, jnp.where((lane >= west_at) & (lane < west_at + HALO), w, 0.0)
                    )
                    for t in range(cols // LANE):
                        joined[p, h, i, :, t * LANE : (t + 1) * LANE] = natural[t, p, picked, :]
                    joined[p, h, i, :, cols : cols + LANE] = side
        return carry

    lax.fori_loop(0, depth, join, 0)

    half_rows = depth * SUB
    wide = cols + LANE
    low_lanes = lax.broadcasted_iota(jnp.int32, (half_rows, LANE), 1) < HALF

    each = range(tiles)
    edge = 2

    def back(x):
        return pltpu.roll(x, 1, 1)

    def ahead(x):
        return pltpu.roll(x, LANE - 1, 1)

    def publish(buf, p, j, row):
        for c in each:
            buf[p, j + 2, c + edge] = row[c]
        buf[p, j + 2, 0] = back(row[-2])
        buf[p, j + 2, 1] = back(row[-1])
        buf[p, j + 2, tiles + edge] = ahead(row[0])
        buf[p, j + 2, tiles + edge + 1] = ahead(row[1])
        if j < 2:
            for c in each:
                x = pltpu.roll(row[c], HALF, 1)
                buf[p, depth + 2 + j, c + edge] = jnp.where(lower_half, x, pltpu.roll(x, SUB - 1, 0))
        if j >= depth - 2:
            for c in each:
                x = pltpu.roll(row[c], HALF, 1)
                buf[p, j + 2 - depth, c + edge] = jnp.where(lower_half, pltpu.roll(x, 1, 0), x)

    def tiled(p):
        both = exact_dot(joined[p].reshape(SIDE * half_rows, wide), to_tiles[...])
        result = []
        for c in each:
            span = slice(c // 2 * LANE, (c // 2 + 1) * LANE)
            a, b = both[:half_rows, span], both[half_rows:, span]
            if c % 2:
                a = pltpu.roll(a, HALF, 1)
            else:
                b = pltpu.roll(b, HALF, 1)
            result.append(jnp.where(low_lanes, a, b))
        return result

    def place(f, carry):
        for k in range(LEVELS):
            p = f * LEVELS + k
            values = tiled(p)
            for j in range(depth):
                publish(first, p, j, [x[j * SUB : (j + 1) * SUB] for x in values])
        return carry

    lax.fori_loop(0, FIELDS, place, 0)
    for p in range(LEVELS + 1):
        for c, value in enumerate(tiled(STATE + p)):
            mix[p, :, c] = value.reshape(depth, SUB, LANE)
    mix[LEVELS] = TIMESTEP * mix[LEVELS]

    def face(before, a, b, after):
        return 7.0 * (a + b) - (before + after)

    def weigh(q):
        for j in range(-1, depth + 1):
            beside = 1 if 0 <= j < depth else 0
            for c in range(-beside, tiles + beside):
                running = None
                for k in range(LEVELS):
                    density = (
                        (-THERMAL * 0.5 * GRAVITY) * q[k, j + 2, c + edge]
                        + (HALINE * 0.5 * GRAVITY) * q[LEVELS + k, j + 2, c + edge]
                    )
                    running = density if running is None else running + density
                    press[k, j + 1, c + 1] = running

    def advance(q, new):
        weigh(q)

        def level(k, carry):
            zonal, merid = 2 * LEVELS + k, 3 * LEVELS + k
            above, under = jnp.maximum(k - 1, 0), jnp.minimum(k + 1, LEVELS - 1)
            for j in range(depth + 1):
                for c in each:
                    fast[j, c] = (q[merid, j + 1, c + edge] + q[merid, j + 2, c + edge]) * (1.0 / 24.0)
            for j in range(depth):
                for c in range(tiles + 1):
                    along[j, c] = (q[zonal, j + 2, c + 1] + q[zonal, j + 2, c + 2]) * (1.0 / 24.0)
            for f in range(FIELDS):
                p = f * LEVELS + k

                def line(j, p=p):
                    return [q[p, j + 2, c + edge] for c in each]

                lines = {j: line(j) for j in (-2, -1, 0)}
                lower = None
                for j in range(-1, depth):
                    lines[j + 2] = line(j + 2)
                    prev, here, succ, succ2 = (lines[j + d] for d in (-1, 0, 1, 2))
                    upper = [fast[j + 1, c] * face(prev[c], here[c], succ[c], succ2[c]) for c in each]
                    if j < 0:
                        lower = upper
                        continue
                    ring = (
                        [q[p, j + 2, 0], q[p, j + 2, 1]]
                        + here
                        + [q[p, j + 2, tiles + edge], q[p, j + 2, tiles + edge + 1]]
                    )
                    flux = [
                        along[j, c] * face(ring[c], ring[c + 1], ring[c + 2], ring[c + 3])
                        for c in range(tiles + 1)
                    ]
                    row = []
                    for c in each:
                        center = here[c]
                        advection = (flux[c + 1] - flux[c]) + (upper[c] - lower[c])
                        around = (ring[c + 1] + ring[c + 3]) + (prev[c] + succ[c])
                        if f < 2:
                            others = q[f * LEVELS + above, j + 2, c + edge] + q[f * LEVELS + under, j + 2, c + edge]
                            mixed = around + (0.5 * others - 5.0 * center)
                        else:
                            mixed = around - 4.0 * center
                        tendency = mix[k, j, c] * mixed - advection
                        if f == 2:
                            slope = press[k, j + 1, c + 2] - press[k, j + 1, c]
                            tendency = tendency + (spin[j] * q[merid, j + 2, c + edge] - slope)
                        elif f == 3:
                            slope = press[k, j + 2, c + 1] - press[k, j, c + 1]
                            tendency = tendency - (spin[j] * q[zonal, j + 2, c + edge] + slope)
                        row.append(center + mix[LEVELS, j, c] * tendency)
                    publish(new, p, j, row)
                    lower = upper
            return carry

        lax.fori_loop(0, LEVELS, level, 0)

    def pair(i, carry):
        advance(first, second)
        advance(second, first)
        return carry

    lax.fori_loop(0, STEPS // 2, pair, 0)

    def gather(f, carry):
        for k in range(LEVELS):
            collect(f, k, f * LEVELS + k)
        return carry

    def collect(f, k, p):
        value = [first[p, 2 : depth + 2, c + edge].reshape(half_rows, LANE) for c in each]
        halves = []
        for h in range(SIDE):
            parts = []
            for c in range(0, tiles, 2):
                a = value[c] if h == 0 else pltpu.roll(value[c], HALF, 1)
                if c + 1 < tiles:
                    b = value[c + 1] if h == 1 else pltpu.roll(value[c + 1], HALF, 1)
                else:
                    b = jnp.zeros_like(a)
                parts.append(jnp.where(low_lanes, a, b))
            halves.append(jnp.concatenate(parts, axis=1))
        flat = exact_dot(jnp.concatenate(halves, axis=0), from_tiles[...])
        for h in range(SIDE):
            for i in range(depth):
                at = (h * depth + i) * SUB
                for t in range(cols // LANE):
                    result[t, f, k, pl.ds(h * depth + i, SUB, stride=SIDE * depth), :] = flat[
                        at : at + SUB, t * LANE : (t + 1) * LANE
                    ]

    lax.fori_loop(0, FIELDS, gather, 0)
    stores = [
        pltpu.make_async_copy(
            result.at[t, :, :, middle, :], out.at[:, :, :, pl.ds(t * LANE, LANE)], out_sem.at[t]
        )
        for t in range(cols // LANE)
    ]
    for c in stores:
        c.start()
    for c in stores:
        c.wait()


def body(lons, lats, ocean_state, mixing, land_sea):
    rows, cols = land_sea.shape
    ext, wide = rows + 2 * HALO, cols + LANE
    depth = ext // (SUB * SIDE)
    tiles = -(-(cols + 2 * HALO) // HALF)
    f32 = jnp.float32
    vmem = pl.BlockSpec(memory_space=pltpu.VMEM)
    hbm = pl.BlockSpec(memory_space=pltpu.HBM)
    lane_tiles = cols // LANE
    extended = pl.pallas_call(
        functools.partial(exchange_kernel, lons, lats),
        out_shape=[
            jax.ShapeDtypeStruct((lane_tiles, PLANES, ext, LANE), f32),
            jax.ShapeDtypeStruct((GROUPS, ext, LANE), f32),
            jax.ShapeDtypeStruct((GROUPS, ext, LANE), f32),
            jax.ShapeDtypeStruct((wide, wide), jnp.bfloat16),
            jax.ShapeDtypeStruct((wide, cols), jnp.bfloat16),
            jax.ShapeDtypeStruct((depth, SUB, LANE), f32),
        ],
        in_specs=[hbm] * 3,
        out_specs=[vmem] * 6,
        scratch_shapes=[
            pltpu.VMEM((GROUPS, rows, LANE), f32),
            pltpu.VMEM((GROUPS, rows, LANE), f32),
            pltpu.VMEM((lane_tiles, PLANES, HALO, LANE), f32),
            pltpu.VMEM((GROUPS, HALO, LANE), f32),
            pltpu.VMEM((GROUPS, HALO, LANE), f32),
            pltpu.VMEM((rows, cols), jnp.int32),
            pltpu.SemaphoreType.DMA((8,)),
            pltpu.SemaphoreType.DMA((8,)),
            pltpu.SemaphoreType.DMA((2,)),
            pltpu.SemaphoreType.DMA((1 + lane_tiles * (FIELDS + 1),)),
        ],
        compiler_params=pltpu.CompilerParams(
            collective_id=0, has_side_effects=True, vmem_limit_bytes=24 * 2**20
        ),
        name="exchange",
    )(ocean_state, mixing, land_sea)
    return pl.pallas_call(
        substeps_kernel,
        out_shape=jax.ShapeDtypeStruct(ocean_state.shape, f32),
        in_specs=[vmem] * 6,
        out_specs=hbm,
        scratch_shapes=[
            pltpu.VMEM((PLANES, SIDE, depth, SUB, wide), f32),
            pltpu.VMEM((STATE, depth + 4, tiles + 4, SUB, LANE), f32),
            pltpu.VMEM((STATE, depth + 4, tiles + 4, SUB, LANE), f32),
            pltpu.VMEM((LEVELS + 1, depth, tiles, SUB, LANE), f32),
            pltpu.VMEM((depth + 1, tiles, SUB, LANE), f32),
            pltpu.VMEM((depth, tiles + 1, SUB, LANE), f32),
            pltpu.VMEM((LEVELS, depth + 2, tiles + 2, SUB, LANE), f32),
            pltpu.VMEM((lane_tiles, FIELDS, LEVELS, ext, LANE), f32),
            pltpu.SemaphoreType.DMA((lane_tiles,)),
        ],
        compiler_params=pltpu.CompilerParams(vmem_limit_bytes=32 * 2**20),
        name="substeps",
    )(*extended)


def solution(mesh):
    in_specs = (P(None, None, "lat", "lon"), P(None, "lat", "lon"), P("lat", "lon"))
    out_specs = P(None, None, "lat", "lon")
    run = functools.partial(body, mesh.shape["lon"], mesh.shape["lat"])
    return jax.shard_map(run, mesh=mesh, in_specs=in_specs, out_specs=out_specs, check_vma=False)
```

```python
import functools

import jax
import jax.numpy as jnp
from jax import lax
from jax.experimental import pallas as pl
from jax.experimental.pallas import tpu as pltpu
from jax.sharding import PartitionSpec as P

STEPS = 8
HALO = 2 * STEPS
FIELDS = 4
LEVELS = 3
STATE = FIELDS * LEVELS
PLANES = STATE + LEVELS + 1
SUB = 8
LANE = 128
PER_TILE = LANE // HALO
GROUPS = PLANES // PER_TILE
SIDE = 2
HALF = LANE // SIDE

THERMAL = 0.2
HALINE = 0.15
GRAVITY = 0.5
TIMESTEP = 0.1


def split3(x):
    high = x.astype(jnp.bfloat16)
    rest = x - high.astype(jnp.float32)
    mid = rest.astype(jnp.bfloat16)
    low = (rest - mid.astype(jnp.float32)).astype(jnp.bfloat16)
    return high, mid, low


def flipped(block):
    x, span = block
    rows, cols = x.shape

    def reversal(size, group):
        i = lax.broadcasted_iota(jnp.int32, (size, size), 0)
        j = lax.broadcasted_iota(jnp.int32, (size, size), 1)
        return jnp.where(j == (i ^ (group - 1)), 1.0, 0.0).astype(jnp.bfloat16)

    def dot(a, b):
        return jnp.dot(a, b, preferred_element_type=jnp.float32)

    flip_lanes = reversal(cols, span)
    flip_rows = reversal(rows, HALO)
    high, mid, low = split3(x)
    x = (dot(high, flip_lanes) + dot(mid, flip_lanes)) + dot(low, flip_lanes)
    high, mid, low = split3(x)
    return (dot(flip_rows, high) + dot(flip_rows, mid)) + dot(flip_rows, low)


def exchange_kernel(
    lons, lats, state, mixing, land, natural, west, east, to_tiles, from_tiles, spin,
    to_west, to_east, to_north, corner_west, corner_east, land_here, send_sem, recv_sem, keep_sem, load_sem,
):
    rows, cols = land.shape
    ext = rows + 2 * HALO
    lon = lax.axis_index("lon")
    lat = lax.axis_index("lat")
    northmost = lat == lats - 1
    has_south = lat > 0
    left = lax.rem(lon + lons - 1, lons)
    right = lax.rem(lon + 1, lons)
    across = lons - 1 - lon
    across_east = lax.rem(2 * lons - 2 - lon, lons)
    across_west = lax.rem(lons - lon, lons)

    low = pl.ds(0, HALO)
    high = pl.ds(ext - HALO, HALO)
    middle = pl.ds(HALO, rows)
    lane_tiles = cols // LANE

    loads = [pltpu.make_async_copy(land, land_here, load_sem.at[0])]
    for t in range(lane_tiles):
        span = pl.ds(t * LANE, LANE)
        for f in range(FIELDS):
            loads.append(
                pltpu.make_async_copy(
                    state.at[f, :, :, span],
                    natural.at[t, pl.ds(f * LEVELS, LEVELS), middle, :],
                    load_sem.at[len(loads)],
                )
            )
        loads.append(
            pltpu.make_async_copy(
                mixing.at[:, :, span], natural.at[t, pl.ds(STATE, LEVELS), middle, :], load_sem.at[len(loads)]
            )
        )
    for c in loads:
        c.start()

    barrier = pltpu.get_barrier_semaphore()

    def greet(x, y):
        pl.semaphore_signal(barrier, inc=1, device_id=(x, y), device_id_type=pl.DeviceIdType.MESH)

    greet(left, lat)
    greet(right, lat)

    @pl.when(has_south)
    def _():
        for x in (left, lon, right):
            greet(x, lat - 1)

    @pl.when(jnp.logical_not(northmost))
    def _():
        for x in (left, lon, right):
            greet(x, lat + 1)

    @pl.when(northmost)
    def _():
        greet(across, lat)

        @pl.when(across_east != lon)
        def _():
            greet(across_east, lat)

        @pl.when(across_west != lon)
        def _():
            greet(across_west, lat)

    for c in loads:
        c.wait()
    for t in range(lane_tiles):
        natural[t, PLANES - 1, HALO : HALO + rows, :] = land_here[:, t * LANE : (t + 1) * LANE].astype(jnp.float32)

    @pl.when(northmost)
    def _():
        top = [natural[t, :, rows : rows + HALO, :].reshape(PLANES * HALO, LANE) for t in range(lane_tiles)]
        full = jnp.concatenate(top, axis=1)
        index = lax.broadcasted_iota(jnp.int32, full.shape, 0) >> (HALO.bit_length() - 1)
        odd = (index >= 2 * LEVELS) & (index < STATE)
        full = flipped((full, cols))
        full = jnp.where(odd, -full, full)
        for t in range(lane_tiles):
            to_north[t] = full[:, t * LANE : (t + 1) * LANE].reshape(PLANES, HALO, LANE)
    @pl.when(has_south & jnp.logical_not(northmost))
    def _():
        pl.semaphore_wait(barrier, 8)

    @pl.when(jnp.logical_not(has_south) & jnp.logical_not(northmost))
    def _():
        pl.semaphore_wait(barrier, 5)

    @pl.when(northmost)
    def _():
        folds = (
            1
            + (across_east != lon).astype(jnp.int32)
            + (across_west != lon).astype(jnp.int32)
        )
        pl.semaphore_wait(barrier, 2 + 3 * has_south.astype(jnp.int32) + folds)

    def copy(src, dst, send, recv, x, y):
        return pltpu.make_async_remote_copy(
            src_ref=src,
            dst_ref=dst,
            send_sem=send_sem.at[send],
            recv_sem=recv_sem.at[recv],
            device_id=(x, y),
            device_id_type=pl.DeviceIdType.MESH,
        )

    def westward():
        return copy(to_west, east.at[:, middle, :], 0, 1, left, lat)

    def eastward():
        return copy(to_east, west.at[:, middle, :], 1, 0, right, lat)

    def southward():
        return (
            copy(natural.at[:, :, pl.ds(HALO, HALO), :], natural.at[:, :, high, :], 2, 2, lon, lat - 1),
            copy(to_west.at[:, low, :], east.at[:, high, :], 3, 3, left, lat - 1),
            copy(to_east.at[:, low, :], west.at[:, high, :], 4, 4, right, lat - 1),
        )

    def northward():
        return (
            copy(natural.at[:, :, pl.ds(rows, HALO), :], natural.at[:, :, low, :], 5, 5, lon, lat + 1),
            copy(corner_west, east.at[:, low, :], 6, 6, left, lat + 1),
            copy(corner_east, west.at[:, low, :], 7, 7, right, lat + 1),
        )

    def folded():
        return copy(to_north, natural.at[:, :, high, :], 5, 2, across, lat)

    def folded_east():
        return copy(corner_east, east.at[:, high, :], 6, 3, across_east, lat)

    def folded_west():
        return copy(corner_west, west.at[:, high, :], 7, 4, across_west, lat)

    def kept_east():
        return pltpu.make_async_copy(corner_east, east.at[:, high, :], keep_sem.at[0])

    def kept_west():
        return pltpu.make_async_copy(corner_west, west.at[:, high, :], keep_sem.at[1])

    @pl.when(northmost)
    def _():
        folded().start()

    @pl.when(has_south)
    def _():
        southward()[0].start()

    @pl.when(jnp.logical_not(northmost))
    def _():
        northward()[0].start()

    lane = lax.broadcasted_iota(jnp.int32, (rows, LANE), 1)
    for g in range(GROUPS):
        packed_west = jnp.zeros((rows, LANE), jnp.float32)
        packed_east = jnp.zeros((rows, LANE), jnp.float32)
        for slot in range(PER_TILE):
            p = g * PER_TILE + slot
            here = (lane >= slot * HALO) & (lane < (slot + 1) * HALO)
            first = natural[0, p, HALO : HALO + rows, :]
            last = natural[lane_tiles - 1, p, HALO : HALO + rows, :]
            if slot:
                first = pltpu.roll(first, slot * HALO, 1)
            if (slot + 1) * HALO != LANE:
                last = pltpu.roll(last, (slot + 1) * HALO, 1)
            packed_west = jnp.where(here, first, packed_west)
            packed_east = jnp.where(here, last, packed_east)
        to_west[g] = packed_west
        to_east[g] = packed_east

    westward().start()
    eastward().start()

    @pl.when(northmost)
    def _():
        shape = (GROUPS * HALO, LANE)
        index = (
            lax.broadcasted_iota(jnp.int32, shape, 0) // HALO * PER_TILE
            + lax.broadcasted_iota(jnp.int32, shape, 1) // HALO
        )
        odd = (index >= 2 * LEVELS) & (index < STATE)
        for source, corner in ((to_west, corner_west), (to_east, corner_east)):
            strip = flipped((source[:, rows - HALO :, :].reshape(shape), HALO))
            corner[...] = jnp.where(odd, -strip, strip).reshape(GROUPS, HALO, LANE)

    @pl.when(jnp.logical_not(northmost))
    def _():
        corner_west[...] = to_west[:, rows - HALO :, :]
        corner_east[...] = to_east[:, rows - HALO :, :]

    @pl.when(has_south)
    def _():
        for c in southward()[1:]:
            c.start()

    @pl.when(jnp.logical_not(northmost))
    def _():
        for c in northward()[1:]:
            c.start()

    @pl.when(northmost)
    def _():
        @pl.when(across_east != lon)
        def _():
            folded_east().start()

        @pl.when(across_east == lon)
        def _():
            kept_east().start()

        @pl.when(across_west != lon)
        def _():
            folded_west().start()

        @pl.when(across_west == lon)
        def _():
            kept_west().start()

    @pl.when(jnp.logical_not(has_south))
    def _():
        natural[:, :, 0:HALO, :] = jnp.zeros((lane_tiles, PLANES, HALO, LANE), jnp.float32)
        west[:, 0:HALO, :] = jnp.zeros((GROUPS, HALO, LANE), jnp.float32)
        east[:, 0:HALO, :] = jnp.zeros((GROUPS, HALO, LANE), jnp.float32)

    tiles = -(-(cols + 2 * HALO) // HALF)
    depth = spin.shape[0]
    def selection(shape, tile_dim):
        j = lax.broadcasted_iota(jnp.int32, shape, tile_dim)
        n = lax.broadcasted_iota(jnp.int32, shape, 1 - tile_dim)
        home = tiles * (j & (HALF - 1)) + (j >> (HALF.bit_length() - 1)) - HALO
        home = jnp.where(home < 0, home + tiles * HALF, home)
        return jnp.where((n == home) & (j < tiles * HALF), 1.0, 0.0).astype(jnp.bfloat16)

    to_tiles[...] = selection(to_tiles.shape, 1)
    from_tiles[...] = selection(from_tiles.shape, 0)

    r = lax.broadcasted_iota(jnp.int32, (depth, SUB, LANE), 0)
    s = lax.broadcasted_iota(jnp.int32, (depth, SUB, LANE), 1)
    h = lax.broadcasted_iota(jnp.int32, (depth, SUB, LANE), 2) >> (HALF.bit_length() - 1)
    total = rows * lats
    row = lat * rows - HALO + (SIDE * s + h) * depth + r
    row = jnp.where(row >= total, 2 * total - 1 - row, row).astype(jnp.float32)
    spin[...] = jnp.sin(jnp.pi * (row + 0.5) / total - jnp.pi / 2)

    westward().wait()
    eastward().wait()

    @pl.when(has_south)
    def _():
        for c in southward():
            c.wait_send()
        for c in northward():
            c.wait_recv()

    @pl.when(jnp.logical_not(northmost))
    def _():
        for c in northward():
            c.wait_send()
        for c in southward():
            c.wait_recv()

    @pl.when(northmost)
    def _():
        folded().wait()

        @pl.when(across_east != lon)
        def _():
            folded_east().wait()

        @pl.when(across_east == lon)
        def _():
            kept_east().wait()

        @pl.when(across_west != lon)
        def _():
            folded_west().wait()

        @pl.when(across_west == lon)
        def _():
            kept_west().wait()


def exact_dot(x, selection):
    rows = x.shape[0]
    pieces = jnp.concatenate(split3(x), axis=0)
    y = jnp.dot(pieces, selection, preferred_element_type=jnp.float32)
    return (y[:rows] + y[rows : 2 * rows]) + y[2 * rows :]


def substeps_kernel(
    natural, west, east, to_tiles, from_tiles, spin, out,
    joined, first, second, mix, fast, along, press, result, out_sem,
):
    lane_tiles, _, ext, _ = natural.shape
    rows, cols = ext - 2 * HALO, lane_tiles * LANE
    depth = spin.shape[0]
    tiles = mix.shape[2]
    lane = lax.broadcasted_iota(jnp.int32, (SUB, LANE), 1)
    lower_half = lane < HALF
    west_at = tiles * HALF - cols - HALO

    def join(i, carry):
        for h in range(SIDE):
            picked = pl.ds(h * depth + i, SUB, stride=SIDE * depth)
            for g in range(GROUPS):
                e_all, w_all = east[g, picked, :], west[g, picked, :]
                for slot in range(PER_TILE):
                    p = g * PER_TILE + slot
                    e, w = e_all, w_all
                    if slot:
                        e = pltpu.roll(e, LANE - slot * HALO, 1)
                    if (west_at - slot * HALO) % LANE:
                        w = pltpu.roll(w, (west_at - slot * HALO) % LANE, 1)
                    side = jnp.where(
                        lane < HALO, e, jnp.where((lane >= west_at) & (lane < west_at + HALO), w, 0.0)
                    )
                    for t in range(cols // LANE):
                        joined[p, h, i, :, t * LANE : (t + 1) * LANE] = natural[t, p, picked, :]
                    joined[p, h, i, :, cols : cols + LANE] = side
        return carry

    lax.fori_loop(0, depth, join, 0)

    half_rows = depth * SUB
    wide = cols + LANE
    low_lanes = lax.broadcasted_iota(jnp.int32, (half_rows, LANE), 1) < HALF

    each = range(tiles)
    edge = 2

    def back(x):
        return pltpu.roll(x, 1, 1)

    def ahead(x):
        return pltpu.roll(x, LANE - 1, 1)

    def publish(buf, p, j, row):
        for c in each:
            buf[p, j + 2, c + edge] = row[c]
        buf[p, j + 2, 0] = back(row[-2])
        buf[p, j + 2, 1] = back(row[-1])
        buf[p, j + 2, tiles + edge] = ahead(row[0])
        buf[p, j + 2, tiles + edge + 1] = ahead(row[1])
        if j < 2:
            for c in each:
                x = pltpu.roll(row[c], HALF, 1)
                buf[p, depth + 2 + j, c + edge] = jnp.where(lower_half, x, pltpu.roll(x, SUB - 1, 0))
        if j >= depth - 2:
            for c in each:
                x = pltpu.roll(row[c], HALF, 1)
                buf[p, j + 2 - depth, c + edge] = jnp.where(lower_half, pltpu.roll(x, 1, 0), x)

    def tiled(p):
        both = exact_dot(joined[p].reshape(SIDE * half_rows, wide), to_tiles[...])
        result = []
        for c in each:
            span = slice(c // 2 * LANE, (c // 2 + 1) * LANE)
            a, b = both[:half_rows, span], both[half_rows:, span]
            if c % 2:
                a = pltpu.roll(a, HALF, 1)
            else:
                b = pltpu.roll(b, HALF, 1)
            result.append(jnp.where(low_lanes, a, b))
        return result

    def place(f, carry):
        for k in range(LEVELS):
            p = f * LEVELS + k
            values = tiled(p)
            for j in range(depth):
                publish(first, p, j, [x[j * SUB : (j + 1) * SUB] for x in values])
        return carry

    lax.fori_loop(0, FIELDS, place, 0)
    for p in range(LEVELS + 1):
        for c, value in enumerate(tiled(STATE + p)):
            mix[p, :, c] = value.reshape(depth, SUB, LANE)
    mix[LEVELS] = TIMESTEP * mix[LEVELS]

    def weigh(q):
        for j in range(-1, depth + 1):
            beside = 1 if 0 <= j < depth else 0
            for c in range(-beside, tiles + beside):
                running = None
                for k in range(LEVELS):
                    density = (
                        (-THERMAL * 0.5 * GRAVITY) * q[k, j + 2, c + edge]
                        + (HALINE * 0.5 * GRAVITY) * q[LEVELS + k, j + 2, c + edge]
                    )
                    running = density if running is None else running + density
                    press[k, j + 1, c + 1] = running

    def advance(q, new):
        weigh(q)

        def level(k, carry):
            zonal, merid = 2 * LEVELS + k, 3 * LEVELS + k
            above, under = jnp.maximum(k - 1, 0), jnp.minimum(k + 1, LEVELS - 1)
            for j in range(depth + 1):
                for c in each:
                    fast[j, c] = (q[merid, j + 1, c + edge] + q[merid, j + 2, c + edge]) * (1.0 / 3.0)
            for j in range(depth):
                for c in range(tiles + 1):
                    along[j, c] = (q[zonal, j + 2, c + 1] + q[zonal, j + 2, c + 2]) * (1.0 / 3.0)
            for f in range(FIELDS):
                p = f * LEVELS + k

                def line(j, p=p):
                    return [q[p, j + 2, c + edge] for c in each]

                lines = {j: line(j) for j in (-2, -1, 0)}
                near = {-1: [lines[-2][c] + lines[0][c] for c in each]}
                bent = {-1: [lines[-1][c] - 0.125 * near[-1][c] for c in each]}
                lower = None
                for j in range(-1, depth):
                    lines[j + 2] = line(j + 2)
                    here = lines[j]
                    near[j + 1] = [lines[j][c] + lines[j + 2][c] for c in each]
                    bent[j + 1] = [lines[j + 1][c] - 0.125 * near[j + 1][c] for c in each]
                    upper = [fast[j + 1, c] * (bent[j][c] + bent[j + 1][c]) for c in each]
                    if j < 0:
                        lower = upper
                        continue
                    ring = (
                        [q[p, j + 2, 0], q[p, j + 2, 1]]
                        + here
                        + [q[p, j + 2, tiles + edge], q[p, j + 2, tiles + edge + 1]]
                    )
                    beside = [ring[c] + ring[c + 2] for c in range(tiles + 2)]
                    curved = [ring[c + 1] - 0.125 * beside[c] for c in range(tiles + 2)]
                    flux = [along[j, c] * (curved[c] + curved[c + 1]) for c in range(tiles + 1)]
                    row = []
                    for c in each:
                        center = here[c]
                        advection = (flux[c + 1] - flux[c]) + (upper[c] - lower[c])
                        around = beside[c + 1] + near[j][c]
                        if f < 2:
                            others = q[f * LEVELS + above, j + 2, c + edge] + q[f * LEVELS + under, j + 2, c + edge]
                            mixed = around + (0.5 * others - 5.0 * center)
                        else:
                            mixed = around - 4.0 * center
                        tendency = mix[k, j, c] * mixed - advection
                        if f == 2:
                            slope = press[k, j + 1, c + 2] - press[k, j + 1, c]
                            tendency = tendency + (spin[j] * q[merid, j + 2, c + edge] - slope)
                        elif f == 3:
                            slope = press[k, j + 2, c + 1] - press[k, j, c + 1]
                            tendency = tendency - (spin[j] * q[zonal, j + 2, c + edge] + slope)
                        row.append(center + mix[LEVELS, j, c] * tendency)
                    publish(new, p, j, row)
                    lower = upper
            return carry

        lax.fori_loop(0, LEVELS, level, 0)

    def pair(i, carry):
        advance(first, second)
        advance(second, first)
        return carry

    lax.fori_loop(0, STEPS // 2, pair, 0)

    def stores(f):
        return [
            pltpu.make_async_copy(
                result.at[t, f, :, pl.ds(HALO, rows), :],
                out.at[f, :, :, pl.ds(t * LANE, LANE)],
                out_sem.at[t, f],
            )
            for t in range(lane_tiles)
        ]

    def gather(f, carry):
        for k in range(LEVELS):
            collect(f, k, f * LEVELS + k)
        for c in stores(f):
            c.start()
        return carry

    def collect(f, k, p):
        value = [first[p, 2 : depth + 2, c + edge].reshape(half_rows, LANE) for c in each]
        halves = []
        for h in range(SIDE):
            parts = []
            for c in range(0, tiles, 2):
                a = value[c] if h == 0 else pltpu.roll(value[c], HALF, 1)
                if c + 1 < tiles:
                    b = value[c + 1] if h == 1 else pltpu.roll(value[c + 1], HALF, 1)
                else:
                    b = jnp.zeros_like(a)
                parts.append(jnp.where(low_lanes, a, b))
            halves.append(jnp.concatenate(parts, axis=1))
        flat = exact_dot(jnp.concatenate(halves, axis=0), from_tiles[...])
        for h in range(SIDE):
            for i in range(depth):
                at = (h * depth + i) * SUB
                for t in range(cols // LANE):
                    result[t, f, k, pl.ds(h * depth + i, SUB, stride=SIDE * depth), :] = flat[
                        at : at + SUB, t * LANE : (t + 1) * LANE
                    ]

    lax.fori_loop(0, FIELDS, gather, 0)
    for f in range(FIELDS):
        for c in stores(f):
            c.wait()


def body(lons, lats, ocean_state, mixing, land_sea):
    rows, cols = land_sea.shape
    ext, wide = rows + 2 * HALO, cols + LANE
    depth = ext // (SUB * SIDE)
    tiles = -(-(cols + 2 * HALO) // HALF)
    f32 = jnp.float32
    vmem = pl.BlockSpec(memory_space=pltpu.VMEM)
    hbm = pl.BlockSpec(memory_space=pltpu.HBM)
    lane_tiles = cols // LANE
    extended = pl.pallas_call(
        functools.partial(exchange_kernel, lons, lats),
        out_shape=[
            jax.ShapeDtypeStruct((lane_tiles, PLANES, ext, LANE), f32),
            jax.ShapeDtypeStruct((GROUPS, ext, LANE), f32),
            jax.ShapeDtypeStruct((GROUPS, ext, LANE), f32),
            jax.ShapeDtypeStruct((wide, wide), jnp.bfloat16),
            jax.ShapeDtypeStruct((wide, cols), jnp.bfloat16),
            jax.ShapeDtypeStruct((depth, SUB, LANE), f32),
        ],
        in_specs=[hbm] * 3,
        out_specs=[vmem] * 6,
        scratch_shapes=[
            pltpu.VMEM((GROUPS, rows, LANE), f32),
            pltpu.VMEM((GROUPS, rows, LANE), f32),
            pltpu.VMEM((lane_tiles, PLANES, HALO, LANE), f32),
            pltpu.VMEM((GROUPS, HALO, LANE), f32),
            pltpu.VMEM((GROUPS, HALO, LANE), f32),
            pltpu.VMEM((rows, cols), jnp.int32),
            pltpu.SemaphoreType.DMA((8,)),
            pltpu.SemaphoreType.DMA((8,)),
            pltpu.SemaphoreType.DMA((2,)),
            pltpu.SemaphoreType.DMA((1 + lane_tiles * (FIELDS + 1),)),
        ],
        compiler_params=pltpu.CompilerParams(
            collective_id=0, has_side_effects=True, vmem_limit_bytes=24 * 2**20
        ),
        name="exchange",
    )(ocean_state, mixing, land_sea)
    return pl.pallas_call(
        substeps_kernel,
        out_shape=jax.ShapeDtypeStruct(ocean_state.shape, f32),
        in_specs=[vmem] * 6,
        out_specs=hbm,
        scratch_shapes=[
            pltpu.VMEM((PLANES, SIDE, depth, SUB, wide), f32),
            pltpu.VMEM((STATE, depth + 4, tiles + 4, SUB, LANE), f32),
            pltpu.VMEM((STATE, depth + 4, tiles + 4, SUB, LANE), f32),
            pltpu.VMEM((LEVELS + 1, depth, tiles, SUB, LANE), f32),
            pltpu.VMEM((depth + 1, tiles, SUB, LANE), f32),
            pltpu.VMEM((depth, tiles + 1, SUB, LANE), f32),
            pltpu.VMEM((LEVELS, depth + 2, tiles + 2, SUB, LANE), f32),
            pltpu.VMEM((lane_tiles, FIELDS, LEVELS, ext, LANE), f32),
            pltpu.SemaphoreType.DMA((lane_tiles, FIELDS)),
        ],
        compiler_params=pltpu.CompilerParams(vmem_limit_bytes=32 * 2**20),
        name="substeps",
    )(*extended)


def solution(mesh):
    in_specs = (P(None, None, "lat", "lon"), P(None, "lat", "lon"), P("lat", "lon"))
    out_specs = P(None, None, "lat", "lon")
    run = functools.partial(body, mesh.shape["lon"], mesh.shape["lat"])
    return jax.shard_map(run, mesh=mesh, in_specs=in_specs, out_specs=out_specs, check_vma=False)
```

```python
import functools

import jax
import jax.numpy as jnp
from jax import lax
from jax.experimental import pallas as pl
from jax.experimental.pallas import tpu as pltpu
from jax.sharding import PartitionSpec as P

STEPS = 8
HALO = 2 * STEPS
FIELDS = 4
LEVELS = 3
STATE = FIELDS * LEVELS
PLANES = STATE + LEVELS + 1
SUB = 8
LANE = 128
PER_TILE = LANE // HALO
GROUPS = PLANES // PER_TILE
SIDE = 2
HALF = LANE // SIDE

THERMAL = 0.2
HALINE = 0.15
GRAVITY = 0.5
TIMESTEP = 0.1


def split3(x):
    high = x.astype(jnp.bfloat16)
    rest = x - high.astype(jnp.float32)
    mid = rest.astype(jnp.bfloat16)
    low = (rest - mid.astype(jnp.float32)).astype(jnp.bfloat16)
    return high, mid, low


def flipped(block):
    x, span = block
    rows, cols = x.shape

    def reversal(size, group):
        i = lax.broadcasted_iota(jnp.int32, (size, size), 0)
        j = lax.broadcasted_iota(jnp.int32, (size, size), 1)
        return jnp.where(j == (i ^ (group - 1)), 1.0, 0.0).astype(jnp.bfloat16)

    def dot(a, b):
        return jnp.dot(a, b, preferred_element_type=jnp.float32)

    flip_lanes = reversal(cols, span)
    flip_rows = reversal(rows, HALO)
    high, mid, low = split3(x)
    x = (dot(high, flip_lanes) + dot(mid, flip_lanes)) + dot(low, flip_lanes)
    high, mid, low = split3(x)
    return (dot(flip_rows, high) + dot(flip_rows, mid)) + dot(flip_rows, low)


def exchange_kernel(
    lons, lats, state, mixing, land, natural, west, east, to_tiles, from_tiles, spin,
    to_west, to_east, to_north, corner_west, corner_east, land_here, send_sem, recv_sem, keep_sem, load_sem,
):
    rows, cols = land.shape
    ext = rows + 2 * HALO
    lon = lax.axis_index("lon")
    lat = lax.axis_index("lat")
    northmost = lat == lats - 1
    has_south = lat > 0
    left = lax.rem(lon + lons - 1, lons)
    right = lax.rem(lon + 1, lons)
    across = lons - 1 - lon
    across_east = lax.rem(2 * lons - 2 - lon, lons)
    across_west = lax.rem(lons - lon, lons)

    low = pl.ds(0, HALO)
    high = pl.ds(ext - HALO, HALO)
    middle = pl.ds(HALO, rows)
    lane_tiles = cols // LANE

    loads = [pltpu.make_async_copy(land, land_here, load_sem.at[0])]
    for t in range(lane_tiles):
        span = pl.ds(t * LANE, LANE)
        for f in range(FIELDS):
            loads.append(
                pltpu.make_async_copy(
                    state.at[f, :, :, span],
                    natural.at[t, pl.ds(f * LEVELS, LEVELS), middle, :],
                    load_sem.at[len(loads)],
                )
            )
        loads.append(
            pltpu.make_async_copy(
                mixing.at[:, :, span], natural.at[t, pl.ds(STATE, LEVELS), middle, :], load_sem.at[len(loads)]
            )
        )
    for c in loads:
        c.start()

    barrier = pltpu.get_barrier_semaphore()

    def greet(x, y):
        pl.semaphore_signal(barrier, inc=1, device_id=(x, y), device_id_type=pl.DeviceIdType.MESH)

    greet(left, lat)
    greet(right, lat)

    @pl.when(has_south)
    def _():
        for x in (left, lon, right):
            greet(x, lat - 1)

    @pl.when(jnp.logical_not(northmost))
    def _():
        for x in (left, lon, right):
            greet(x, lat + 1)

    @pl.when(northmost)
    def _():
        greet(across, lat)

        @pl.when(across_east != lon)
        def _():
            greet(across_east, lat)

        @pl.when(across_west != lon)
        def _():
            greet(across_west, lat)

    for c in loads:
        c.wait()
    for t in range(lane_tiles):
        natural[t, PLANES - 1, HALO : HALO + rows, :] = land_here[:, t * LANE : (t + 1) * LANE].astype(jnp.float32)

    lane = lax.broadcasted_iota(jnp.int32, (rows, LANE), 1)
    for g in range(GROUPS):
        packed_west = jnp.zeros((rows, LANE), jnp.float32)
        packed_east = jnp.zeros((rows, LANE), jnp.float32)
        for slot in range(PER_TILE):
            p = g * PER_TILE + slot
            here = (lane >= slot * HALO) & (lane < (slot + 1) * HALO)
            first = natural[0, p, HALO : HALO + rows, :]
            last = natural[lane_tiles - 1, p, HALO : HALO + rows, :]
            if slot:
                first = pltpu.roll(first, slot * HALO, 1)
            if (slot + 1) * HALO != LANE:
                last = pltpu.roll(last, (slot + 1) * HALO, 1)
            packed_west = jnp.where(here, first, packed_west)
            packed_east = jnp.where(here, last, packed_east)
        to_west[g] = packed_west
        to_east[g] = packed_east

    @pl.when(northmost)
    def _():
        top = [natural[t, :, rows : rows + HALO, :].reshape(PLANES * HALO, LANE) for t in range(lane_tiles)]
        full = jnp.concatenate(top, axis=1)
        index = lax.broadcasted_iota(jnp.int32, full.shape, 0) >> (HALO.bit_length() - 1)
        odd = (index >= 2 * LEVELS) & (index < STATE)
        full = flipped((full, cols))
        full = jnp.where(odd, -full, full)
        for t in range(lane_tiles):
            to_north[t] = full[:, t * LANE : (t + 1) * LANE].reshape(PLANES, HALO, LANE)
        shape = (GROUPS * HALO, LANE)
        index = (
            lax.broadcasted_iota(jnp.int32, shape, 0) // HALO * PER_TILE
            + lax.broadcasted_iota(jnp.int32, shape, 1) // HALO
        )
        odd = (index >= 2 * LEVELS) & (index < STATE)
        for source, corner in ((to_west, corner_west), (to_east, corner_east)):
            strip = flipped((source[:, rows - HALO :, :].reshape(shape), HALO))
            corner[...] = jnp.where(odd, -strip, strip).reshape(GROUPS, HALO, LANE)

    @pl.when(jnp.logical_not(northmost))
    def _():
        corner_west[...] = to_west[:, rows - HALO :, :]
        corner_east[...] = to_east[:, rows - HALO :, :]

    @pl.when(has_south & jnp.logical_not(northmost))
    def _():
        pl.semaphore_wait(barrier, 8)

    @pl.when(jnp.logical_not(has_south) & jnp.logical_not(northmost))
    def _():
        pl.semaphore_wait(barrier, 5)

    @pl.when(northmost)
    def _():
        folds = (
            1
            + (across_east != lon).astype(jnp.int32)
            + (across_west != lon).astype(jnp.int32)
        )
        pl.semaphore_wait(barrier, 2 + 3 * has_south.astype(jnp.int32) + folds)

    def copy(src, dst, send, recv, x, y):
        return pltpu.make_async_remote_copy(
            src_ref=src,
            dst_ref=dst,
            send_sem=send_sem.at[send],
            recv_sem=recv_sem.at[recv],
            device_id=(x, y),
            device_id_type=pl.DeviceIdType.MESH,
        )

    def westward():
        return copy(to_west, east.at[:, middle, :], 0, 1, left, lat)

    def eastward():
        return copy(to_east, west.at[:, middle, :], 1, 0, right, lat)

    def southward():
        return (
            copy(natural.at[:, :, pl.ds(HALO, HALO), :], natural.at[:, :, high, :], 2, 2, lon, lat - 1),
            copy(to_west.at[:, low, :], east.at[:, high, :], 3, 3, left, lat - 1),
            copy(to_east.at[:, low, :], west.at[:, high, :], 4, 4, right, lat - 1),
        )

    def northward():
        return (
            copy(natural.at[:, :, pl.ds(rows, HALO), :], natural.at[:, :, low, :], 5, 5, lon, lat + 1),
            copy(corner_west, east.at[:, low, :], 6, 6, left, lat + 1),
            copy(corner_east, west.at[:, low, :], 7, 7, right, lat + 1),
        )

    def folded():
        return copy(to_north, natural.at[:, :, high, :], 5, 2, across, lat)

    def folded_east():
        return copy(corner_east, east.at[:, high, :], 6, 3, across_east, lat)

    def folded_west():
        return copy(corner_west, west.at[:, high, :], 7, 4, across_west, lat)

    def kept_east():
        return pltpu.make_async_copy(corner_east, east.at[:, high, :], keep_sem.at[0])

    def kept_west():
        return pltpu.make_async_copy(corner_west, west.at[:, high, :], keep_sem.at[1])

    westward().start()
    eastward().start()

    @pl.when(has_south)
    def _():
        for c in southward():
            c.start()

    @pl.when(jnp.logical_not(northmost))
    def _():
        for c in northward():
            c.start()

    @pl.when(northmost)
    def _():
        folded().start()

        @pl.when(across_east != lon)
        def _():
            folded_east().start()

        @pl.when(across_east == lon)
        def _():
            kept_east().start()

        @pl.when(across_west != lon)
        def _():
            folded_west().start()

        @pl.when(across_west == lon)
        def _():
            kept_west().start()

    @pl.when(jnp.logical_not(has_south))
    def _():
        natural[:, :, 0:HALO, :] = jnp.zeros((lane_tiles, PLANES, HALO, LANE), jnp.float32)
        west[:, 0:HALO, :] = jnp.zeros((GROUPS, HALO, LANE), jnp.float32)
        east[:, 0:HALO, :] = jnp.zeros((GROUPS, HALO, LANE), jnp.float32)

    tiles = -(-(cols + 2 * HALO) // HALF)
    depth = spin.shape[0]
    def selection(shape, tile_dim):
        j = lax.broadcasted_iota(jnp.int32, shape, tile_dim)
        n = lax.broadcasted_iota(jnp.int32, shape, 1 - tile_dim)
        home = tiles * (j & (HALF - 1)) + (j >> (HALF.bit_length() - 1)) - HALO
        home = jnp.where(home < 0, home + tiles * HALF, home)
        return jnp.where((n == home) & (j < tiles * HALF), 1.0, 0.0).astype(jnp.bfloat16)

    to_tiles[...] = selection(to_tiles.shape, 1)
    from_tiles[...] = selection(from_tiles.shape, 0)

    r = lax.broadcasted_iota(jnp.int32, (depth, SUB, LANE), 0)
    s = lax.broadcasted_iota(jnp.int32, (depth, SUB, LANE), 1)
    h = lax.broadcasted_iota(jnp.int32, (depth, SUB, LANE), 2) >> (HALF.bit_length() - 1)
    total = rows * lats
    row = lat * rows - HALO + (SIDE * s + h) * depth + r
    row = jnp.where(row >= total, 2 * total - 1 - row, row).astype(jnp.float32)
    spin[...] = jnp.sin(jnp.pi * (row + 0.5) / total - jnp.pi / 2)

    westward().wait()
    eastward().wait()

    @pl.when(has_south)
    def _():
        for c in southward():
            c.wait_send()
        for c in northward():
            c.wait_recv()

    @pl.when(jnp.logical_not(northmost))
    def _():
        for c in northward():
            c.wait_send()
        for c in southward():
            c.wait_recv()

    @pl.when(northmost)
    def _():
        folded().wait()

        @pl.when(across_east != lon)
        def _():
            folded_east().wait()

        @pl.when(across_east == lon)
        def _():
            kept_east().wait()

        @pl.when(across_west != lon)
        def _():
            folded_west().wait()

        @pl.when(across_west == lon)
        def _():
            kept_west().wait()


def exact_dot(x, selection):
    rows = x.shape[0]
    pieces = jnp.concatenate(split3(x), axis=0)
    y = jnp.dot(pieces, selection, preferred_element_type=jnp.float32)
    return (y[:rows] + y[rows : 2 * rows]) + y[2 * rows :]


def substeps_kernel(
    natural, west, east, to_tiles, from_tiles, spin, out,
    joined, first, second, mix, fast, along, press, result, out_sem,
):
    lane_tiles, _, ext, _ = natural.shape
    rows, cols = ext - 2 * HALO, lane_tiles * LANE
    depth = spin.shape[0]
    tiles = mix.shape[2]
    lane = lax.broadcasted_iota(jnp.int32, (SUB, LANE), 1)
    lower_half = lane < HALF
    west_at = tiles * HALF - cols - HALO

    def join(i, carry):
        for h in range(SIDE):
            picked = pl.ds(h * depth + i, SUB, stride=SIDE * depth)
            for g in range(GROUPS):
                e_all, w_all = east[g, picked, :], west[g, picked, :]
                for slot in range(PER_TILE):
                    p = g * PER_TILE + slot
                    e, w = e_all, w_all
                    if slot:
                        e = pltpu.roll(e, LANE - slot * HALO, 1)
                    if (west_at - slot * HALO) % LANE:
                        w = pltpu.roll(w, (west_at - slot * HALO) % LANE, 1)
                    side = jnp.where(
                        lane < HALO, e, jnp.where((lane >= west_at) & (lane < west_at + HALO), w, 0.0)
                    )
                    for t in range(cols // LANE):
                        joined[p, h, i, :, t * LANE : (t + 1) * LANE] = natural[t, p, picked, :]
                    joined[p, h, i, :, cols : cols + LANE] = side
        return carry

    lax.fori_loop(0, depth, join, 0)

    half_rows = depth * SUB
    wide = cols + LANE
    low_lanes = lax.broadcasted_iota(jnp.int32, (half_rows, LANE), 1) < HALF

    each = range(tiles)
    edge = 2

    def back(x):
        return pltpu.roll(x, 1, 1)

    def ahead(x):
        return pltpu.roll(x, LANE - 1, 1)

    def publish(buf, p, j, row):
        for c in each:
            buf[p, j + 2, c + edge] = row[c]
        buf[p, j + 2, 0] = back(row[-2])
        buf[p, j + 2, 1] = back(row[-1])
        buf[p, j + 2, tiles + edge] = ahead(row[0])
        buf[p, j + 2, tiles + edge + 1] = ahead(row[1])
        if j < 2:
            for c in each:
                x = pltpu.roll(row[c], HALF, 1)
                buf[p, depth + 2 + j, c + edge] = jnp.where(lower_half, x, pltpu.roll(x, SUB - 1, 0))
        if j >= depth - 2:
            for c in each:
                x = pltpu.roll(row[c], HALF, 1)
                buf[p, j + 2 - depth, c + edge] = jnp.where(lower_half, pltpu.roll(x, 1, 0), x)

    def tiled(p):
        both = exact_dot(joined[p].reshape(SIDE * half_rows, wide), to_tiles[...])
        result = []
        for c in each:
            span = slice(c // 2 * LANE, (c // 2 + 1) * LANE)
            a, b = both[:half_rows, span], both[half_rows:, span]
            if c % 2:
                a = pltpu.roll(a, HALF, 1)
            else:
                b = pltpu.roll(b, HALF, 1)
            result.append(jnp.where(low_lanes, a, b))
        return result

    def place(f, carry):
        for k in range(LEVELS):
            p = f * LEVELS + k
            values = tiled(p)
            for j in range(depth):
                publish(first, p, j, [x[j * SUB : (j + 1) * SUB] for x in values])
        return carry

    lax.fori_loop(0, FIELDS, place, 0)
    for p in range(LEVELS + 1):
        for c, value in enumerate(tiled(STATE + p)):
            mix[p, :, c] = value.reshape(depth, SUB, LANE)
    mix[LEVELS] = TIMESTEP * mix[LEVELS]

    def weigh(q):
        for j in range(-1, depth + 1):
            beside = 1 if 0 <= j < depth else 0
            for c in range(-beside, tiles + beside):
                running = None
                for k in range(LEVELS):
                    density = (
                        (-THERMAL * 0.5 * GRAVITY) * q[k, j + 2, c + edge]
                        + (HALINE * 0.5 * GRAVITY) * q[LEVELS + k, j + 2, c + edge]
                    )
                    running = density if running is None else running + density
                    press[k, j + 1, c + 1] = running

    def advance(q, new):
        weigh(q)

        def level(k, carry):
            zonal, merid = 2 * LEVELS + k, 3 * LEVELS + k
            above, under = jnp.maximum(k - 1, 0), jnp.minimum(k + 1, LEVELS - 1)
            for j in range(depth + 1):
                for c in each:
                    fast[j, c] = (q[merid, j + 1, c + edge] + q[merid, j + 2, c + edge]) * (1.0 / 3.0)
            for j in range(depth):
                for c in range(tiles + 1):
                    along[j, c] = (q[zonal, j + 2, c + 1] + q[zonal, j + 2, c + 2]) * (1.0 / 3.0)
            for f in range(FIELDS):
                p = f * LEVELS + k

                def line(j, p=p):
                    return [q[p, j + 2, c + edge] for c in each]

                lines = {j: line(j) for j in (-2, -1, 0)}
                near = {-1: [lines[-2][c] + lines[0][c] for c in each]}
                bent = {-1: [lines[-1][c] - 0.125 * near[-1][c] for c in each]}
                lower = None
                for j in range(-1, depth):
                    lines[j + 2] = line(j + 2)
                    here = lines[j]
                    near[j + 1] = [lines[j][c] + lines[j + 2][c] for c in each]
                    bent[j + 1] = [lines[j + 1][c] - 0.125 * near[j + 1][c] for c in each]
                    upper = [fast[j + 1, c] * (bent[j][c] + bent[j + 1][c]) for c in each]
                    if j < 0:
                        lower = upper
                        continue
                    ring = (
                        [q[p, j + 2, 0], q[p, j + 2, 1]]
                        + here
                        + [q[p, j + 2, tiles + edge], q[p, j + 2, tiles + edge + 1]]
                    )
                    beside = [ring[c] + ring[c + 2] for c in range(tiles + 2)]
                    curved = [ring[c + 1] - 0.125 * beside[c] for c in range(tiles + 2)]
                    flux = [along[j, c] * (curved[c] + curved[c + 1]) for c in range(tiles + 1)]
                    row = []
                    for c in each:
                        center = here[c]
                        advection = (flux[c + 1] - flux[c]) + (upper[c] - lower[c])
                        around = beside[c + 1] + near[j][c]
                        if f < 2:
                            others = q[f * LEVELS + above, j + 2, c + edge] + q[f * LEVELS + under, j + 2, c + edge]
                            mixed = around + (0.5 * others - 5.0 * center)
                        else:
                            mixed = around - 4.0 * center
                        tendency = mix[k, j, c] * mixed - advection
                        if f == 2:
                            slope = press[k, j + 1, c + 2] - press[k, j + 1, c]
                            tendency = tendency + (spin[j] * q[merid, j + 2, c + edge] - slope)
                        elif f == 3:
                            slope = press[k, j + 2, c + 1] - press[k, j, c + 1]
                            tendency = tendency - (spin[j] * q[zonal, j + 2, c + edge] + slope)
                        row.append(center + mix[LEVELS, j, c] * tendency)
                    publish(new, p, j, row)
                    lower = upper
            return carry

        lax.fori_loop(0, LEVELS, level, 0)

    def pair(i, carry):
        advance(first, second)
        advance(second, first)
        return carry

    lax.fori_loop(0, STEPS // 2, pair, 0)

    def stores(f):
        return [
            pltpu.make_async_copy(
                result.at[t, f, :, pl.ds(HALO, rows), :],
                out.at[f, :, :, pl.ds(t * LANE, LANE)],
                out_sem.at[t, f],
            )
            for t in range(lane_tiles)
        ]

    def gather(f, carry):
        for k in range(LEVELS):
            collect(f, k, f * LEVELS + k)
        for c in stores(f):
            c.start()
        return carry

    def collect(f, k, p):
        value = [first[p, 2 : depth + 2, c + edge].reshape(half_rows, LANE) for c in each]
        halves = []
        for h in range(SIDE):
            parts = []
            for c in range(0, tiles, 2):
                a = value[c] if h == 0 else pltpu.roll(value[c], HALF, 1)
                if c + 1 < tiles:
                    b = value[c + 1] if h == 1 else pltpu.roll(value[c + 1], HALF, 1)
                else:
                    b = jnp.zeros_like(a)
                parts.append(jnp.where(low_lanes, a, b))
            halves.append(jnp.concatenate(parts, axis=1))
        flat = exact_dot(jnp.concatenate(halves, axis=0), from_tiles[...])
        for h in range(SIDE):
            for i in range(depth):
                at = (h * depth + i) * SUB
                for t in range(cols // LANE):
                    result[t, f, k, pl.ds(h * depth + i, SUB, stride=SIDE * depth), :] = flat[
                        at : at + SUB, t * LANE : (t + 1) * LANE
                    ]

    lax.fori_loop(0, FIELDS, gather, 0)
    for f in range(FIELDS):
        for c in stores(f):
            c.wait()


def body(lons, lats, ocean_state, mixing, land_sea):
    rows, cols = land_sea.shape
    ext, wide = rows + 2 * HALO, cols + LANE
    depth = ext // (SUB * SIDE)
    tiles = -(-(cols + 2 * HALO) // HALF)
    f32 = jnp.float32
    vmem = pl.BlockSpec(memory_space=pltpu.VMEM)
    hbm = pl.BlockSpec(memory_space=pltpu.HBM)
    lane_tiles = cols // LANE
    extended = pl.pallas_call(
        functools.partial(exchange_kernel, lons, lats),
        out_shape=[
            jax.ShapeDtypeStruct((lane_tiles, PLANES, ext, LANE), f32),
            jax.ShapeDtypeStruct((GROUPS, ext, LANE), f32),
            jax.ShapeDtypeStruct((GROUPS, ext, LANE), f32),
            jax.ShapeDtypeStruct((wide, wide), jnp.bfloat16),
            jax.ShapeDtypeStruct((wide, cols), jnp.bfloat16),
            jax.ShapeDtypeStruct((depth, SUB, LANE), f32),
        ],
        in_specs=[hbm] * 3,
        out_specs=[vmem] * 6,
        scratch_shapes=[
            pltpu.VMEM((GROUPS, rows, LANE), f32),
            pltpu.VMEM((GROUPS, rows, LANE), f32),
            pltpu.VMEM((lane_tiles, PLANES, HALO, LANE), f32),
            pltpu.VMEM((GROUPS, HALO, LANE), f32),
            pltpu.VMEM((GROUPS, HALO, LANE), f32),
            pltpu.VMEM((rows, cols), jnp.int32),
            pltpu.SemaphoreType.DMA((8,)),
            pltpu.SemaphoreType.DMA((8,)),
            pltpu.SemaphoreType.DMA((2,)),
            pltpu.SemaphoreType.DMA((1 + lane_tiles * (FIELDS + 1),)),
        ],
        compiler_params=pltpu.CompilerParams(
            collective_id=0, has_side_effects=True, vmem_limit_bytes=24 * 2**20
        ),
        name="exchange",
    )(ocean_state, mixing, land_sea)
    return pl.pallas_call(
        substeps_kernel,
        out_shape=jax.ShapeDtypeStruct(ocean_state.shape, f32),
        in_specs=[vmem] * 6,
        out_specs=hbm,
        scratch_shapes=[
            pltpu.VMEM((PLANES, SIDE, depth, SUB, wide), f32),
            pltpu.VMEM((STATE, depth + 4, tiles + 4, SUB, LANE), f32),
            pltpu.VMEM((STATE, depth + 4, tiles + 4, SUB, LANE), f32),
            pltpu.VMEM((LEVELS + 1, depth, tiles, SUB, LANE), f32),
            pltpu.VMEM((depth + 1, tiles, SUB, LANE), f32),
            pltpu.VMEM((depth, tiles + 1, SUB, LANE), f32),
            pltpu.VMEM((LEVELS, depth + 2, tiles + 2, SUB, LANE), f32),
            pltpu.VMEM((lane_tiles, FIELDS, LEVELS, ext, LANE), f32),
            pltpu.SemaphoreType.DMA((lane_tiles, FIELDS)),
        ],
        compiler_params=pltpu.CompilerParams(vmem_limit_bytes=32 * 2**20),
        name="substeps",
    )(*extended)


def solution(mesh):
    in_specs = (P(None, None, "lat", "lon"), P(None, "lat", "lon"), P("lat", "lon"))
    out_specs = P(None, None, "lat", "lon")
    run = functools.partial(body, mesh.shape["lon"], mesh.shape["lat"])
    return jax.shard_map(run, mesh=mesh, in_specs=in_specs, out_specs=out_specs, check_vma=False)
```
